32 devices in a mesh: freq: 8 (over z, y), tm: 4 (over x, core).
Axes of the slice: x: 2, y: 2, z: 4, core: 2. Of those that a mesh axis runs over, the one named last changes fastest.
Arguments:
- spectrogram: bfloat16 [4096, 2048], P('freq', 'tm'), may hold values from -6 to 6
- low_share: int32 [127], replicated, may hold values from 24 to 44
- jitter: int32 [254], replicated, may hold values from 0 to 63
Outputs:
- best: float32 [9, 2048], P(None, 'tm')
The draws below stay inside these ranges and needn't reach their ends.
All inputs are finite; a program needn't handle non-finite values.
Results may differ from the reference program's by a relative error of at most 0.0003.
Values sent between devices are 32-bit elements; how exact they have to be, the bound alone decides.
A program may use at most 64 MiB of HBM per device.

```python
import math
import jax
import jax.numpy as jnp
from jax import lax

SUMMED = 32
WIDTHS = 9
CHANNELS = 4096
TRIALS = 128
TIME = 2048


def with_ends(result, own_key, smallest, top_value):
    place = [jax.random.randint(jax.random.fold_in(own_key, axis), (), 0, length) for axis, length in enumerate(result.shape)]
    longest = result.shape.index(max(result.shape))
    next_to = place[:longest] + [(place[longest] + 1) % result.shape[longest]] + place[longest + 1:]
    return result.at[tuple(place)].set(smallest).at[tuple(next_to)].set(top_value)


def steps_of(rng, extent, shards, least, top_value):
    loudness = 1.0
    for dim, blocks in shards:
        heights = jax.random.uniform(jax.random.fold_in(jax.random.fold_in(rng, 6), dim), (blocks,), jnp.float32, least / len(shards), top_value / len(shards))
        loudness = loudness * jnp.repeat(jnp.exp(heights), extent[dim] // blocks).reshape((-1,) + (1,) * (len(extent) - 1 - dim))
    return loudness


def bell_draw(key, shape, deviation, bound, shards=(), kind=jnp.bfloat16):
    values = jax.random.normal(key, shape, jnp.float32) * deviation
    if len(shards) > 0:
        values = steps_of(key, shape, shards, -0.22, 0.18) * values
    return jnp.clip(values, min=-bound, max=bound).astype(kind)


def setup_inputs(seed: int = 0) -> dict:
    streams_of = jax.random.split(jax.random.key(seed), 4)
    return {
        "spectrogram": bell_draw(streams_of[0], (CHANNELS, TIME), 1.0, 6.0, ((0, 8), (1, 4))),
        "low_share": with_ends(jax.random.randint(streams_of[1], (TRIALS - 1,), 24, 45), jax.random.fold_in(streams_of[1], 1), 24, 44).astype(jnp.int32),
        "jitter": with_ends(jax.random.randint(streams_of[2], (2 * TRIALS - 2,), 0, 64), jax.random.fold_in(streams_of[2], 1), 0, 63).astype(jnp.int32),
    }


def shift_table(trial_count, low_share, jitter):
    groups = TRIALS // trial_count
    subband = jnp.arange(groups, dtype=jnp.int32)[:, None]
    trial_ids = jnp.arange(trial_count, dtype=jnp.int32)[None, :]
    rate_rows = jnp.take(low_share, groups - 1 + subband)
    return (trial_ids * rate_rows + jnp.take(jitter, trial_count - 2 + trial_ids)) // 64

def reference(spectrogram, low_share, jitter):
    states = lax.optimization_barrier(jnp.sum(spectrogram.reshape(TRIALS, SUMMED, TIME), axis=1, dtype=jnp.float32))[:, None, :]
    trial_count = 2
    while trial_count <= TRIALS:
        low_rows = jnp.repeat(states[0::2], 2, axis=1)
        high_rows = jnp.repeat(states[1::2], 2, axis=1)
        shifts = shift_table(trial_count, low_share, jitter)
        padded = jnp.pad(high_rows, ((0, 0), (0, 0), (trial_count, 0)))
        index_grid = (trial_count - shifts)[:, :, None] + jnp.arange(TIME, dtype=jnp.int32)[None, None, :]
        states = low_rows + jnp.take_along_axis(padded, index_grid, axis=2)
        trial_count = trial_count * 2
    signal = states[0] / math.sqrt(CHANNELS)
    window = signal
    outputs = []
    width_now = 1
    for level_index in range(WIDTHS):
        outputs.append(lax.optimization_barrier(jnp.max(window, axis=0)) / math.sqrt(width_now))
        window = window + jnp.pad(window, ((0, 0), (width_now, 0)))[:, :TIME]
        width_now = width_now * 2
    return jnp.stack(outputs)
```

```python
import functools
import math

import jax
import jax.numpy as jnp
from jax import lax
from jax.experimental import pallas as pl
from jax.experimental.pallas import tpu as pltpu
from jax.sharding import PartitionSpec as P

SUMMED = 32
WIDTHS = 9
LANES = 128
SUBLANES = 8
MESH = pl.DeviceIdType.MESH


def passed_along(block, axis, distance):
    devices = range(lax.axis_size(axis))
    route = [(i - distance, i) for i in devices if i - distance in devices]
    return lax.ppermute(block, axis, route)


def swapped(block, axis, apart):
    count = lax.axis_size(axis)
    route = []
    for low in range(count):
        high = low | 1 << apart
        if high != low and high < count:
            route += [(low, high), (high, low)]
    return lax.ppermute(block, axis, route)


def widen(trial_rows, fetch_width):
    if fetch_width == 0:
        return trial_rows
    span_time = trial_rows.shape[-1]
    hop_count = min(-(-fetch_width // span_time), lax.axis_size("tm") - 1)
    pieces = [trial_rows]
    fetched = 0
    for hop_index in range(1, hop_count + 1):
        taken_cols = min(span_time, fetch_width - fetched)
        arrived = passed_along(trial_rows[..., span_time - taken_cols :], "tm", hop_index)
        pieces.insert(0, arrived)
        fetched = fetched + taken_cols
    if fetched < fetch_width:
        pieces.insert(
            0, jnp.zeros(trial_rows.shape[:-1] + (fetch_width - fetched,), trial_rows.dtype)
        )
    return jnp.concatenate(pieces, axis=-1)


def align_pair(low_set, high_set, margin, need_now, fetch_width):
    if fetch_width == 0:
        return (low_set[..., need_now:], high_set, margin - need_now)
    high_set = widen(high_set, fetch_width)
    low_set = widen(low_set, fetch_width - need_now)
    return (low_set, high_set, fetch_width - need_now)


def delay_of(trial_ids, subband_ids, trial_count, low_share, jitter):
    all_trials = low_share.shape[0] + 1
    rate_rows = jnp.take(low_share, all_trials // trial_count - 1 + subband_ids)
    return (trial_ids * rate_rows + jnp.take(jitter, trial_count - 2 + trial_ids)) // 64


def merge_rows(low_rows, high_rows, shifts, need_now):
    offsets = need_now - shifts
    bit_count = max(need_now.bit_length(), 1)
    moved = high_rows
    for bit_index in range(bit_count):
        step_size = 2**bit_index
        cols = moved.shape[-1]
        selected = (offsets >> bit_index & 1)[:, None] == 1
        moved = jnp.where(selected, moved[:, step_size:], moved[:, : cols - step_size])
    return low_rows + moved


def shards_any_reach(spectrogram, low_share, jitter):
    trial_dev = spectrogram.shape[0] // SUMMED
    span_time = spectrogram.shape[1]
    all_trials = low_share.shape[0] + 1
    freq_bits = lax.axis_size("freq").bit_length() - 1
    device = lax.axis_index("freq")
    local_counts = []
    trial_count = 2
    while trial_count <= trial_dev:
        local_counts.append(trial_count)
        trial_count = trial_count * 2
    cross_counts = [trial_dev * 2 ** (bit_index + 1) for bit_index in range(freq_bits)]
    need_list = [count_now - 1 for count_now in local_counts + cross_counts] + [
        2 ** (WIDTHS - 1) - 1
    ]
    fetch_plan = []
    margin = 0
    for position in range(len(need_list)):
        need_now = need_list[position]
        if margin >= need_now:
            fetch_plan.append(0)
            margin = margin - need_now
            continue
        fetch_width = need_now
        for later_need in need_list[position + 1 :]:
            if fetch_width + later_need > span_time:
                break
            fetch_width = fetch_width + later_need
        fetch_plan.append(fetch_width)
        margin = fetch_width - need_now
    states = jnp.sum(spectrogram.reshape(trial_dev, SUMMED, span_time), axis=1, dtype=jnp.float32)[
        :, None, :
    ]
    margin = 0
    section_index = 0
    for trial_count in local_counts:
        need_now = trial_count - 1
        groups = states.shape[0] // 2
        low_set, high_set, margin = align_pair(
            states[0::2], states[1::2], margin, need_now, fetch_plan[section_index]
        )
        low_rows = jnp.repeat(low_set, 2, axis=1).reshape(groups * trial_count, -1)
        high_rows = jnp.repeat(high_set, 2, axis=1).reshape(groups * trial_count, -1)
        trial_ids = jnp.tile(jnp.arange(trial_count, dtype=jnp.int32), groups)
        subband_ids = device * (trial_dev // trial_count) + jnp.repeat(
            jnp.arange(groups, dtype=jnp.int32), trial_count
        )
        shifts = delay_of(trial_ids, subband_ids, trial_count, low_share, jitter)
        states = merge_rows(low_rows, high_rows, shifts, need_now).reshape(groups, trial_count, -1)
        section_index = section_index + 1
    trial_rows = states[0]
    trial_ids = jnp.arange(trial_dev, dtype=jnp.int32)
    for bit_index in range(freq_bits):
        trial_count = cross_counts[bit_index]
        need_now = trial_count - 1
        partner = swapped(trial_rows, "freq", bit_index)
        upper_half = device >> bit_index & 1
        low_rows = jnp.where(upper_half == 1, partner, trial_rows)
        high_rows = jnp.where(upper_half == 1, trial_rows, partner)
        low_rows, high_rows, margin = align_pair(
            low_rows, high_rows, margin, need_now, fetch_plan[section_index]
        )
        trial_ids = 2 * trial_ids + upper_half
        shifts = delay_of(trial_ids, device >> bit_index + 1, trial_count, low_share, jitter)
        trial_rows = merge_rows(low_rows, high_rows, shifts, need_now)
        section_index = section_index + 1
    if fetch_plan[section_index] > 0:
        trial_rows = widen(trial_rows, fetch_plan[section_index])
    signal = trial_rows / math.sqrt(all_trials * SUMMED)
    peak_rows = []
    window_sum = signal
    width_now = 1
    for level_index in range(WIDTHS):
        length = window_sum.shape[1]
        peak_rows.append(
            jnp.max(window_sum[:, length - span_time :], axis=0) / math.sqrt(width_now)
        )
        if level_index + 1 < WIDTHS:
            window_sum = window_sum[:, width_now:] + window_sum[:, : length - width_now]
            width_now = width_now * 2
    local_best = jnp.stack(peak_rows)
    return lax.pmax(local_best, "freq")


def moved(row, above, delay, lane):
    return pltpu.roll(jnp.where(lane >= LANES - delay, above, row), delay, 1)


def merged(old, count, first_trial, first_subband, all_trials, share, rest, lane):
    new = []
    for s in range(len(old) // 2):
        rate = share[all_trials // count - 1 + first_subband + s]
        highs = [(row, pltpu.roll(row, 1, 0)) for row in old[2 * s + 1]]
        trials = []
        for j in range(2 * len(highs)):
            trial = first_trial + j
            delay = (trial * rate + rest[count - 2 + trial]) >> 6
            trials.append(old[2 * s][j // 2] + moved(*highs[j // 2], delay, lane))
        new.append(trials)
    return new


def search(
    bands, slots, all_trials,
    spec_hbm, share_hbm, rest_hbm, best_ref,
    spec, share, rest, base_rows, rows, here, before, part, parts, mine, whole,
    in_sem, here_send, here_recv, next_send, next_recv, part_send, part_recv, all_send, all_recv,
):
    k, m = lax.axis_index("freq"), lax.axis_index("tm")
    span = spec.shape[1]
    chunks = span // LANES
    local = spec.shape[0] // SUMMED
    each = local // bands

    loads = [
        pltpu.make_async_copy(spec_hbm, spec, in_sem.at[0]),
        pltpu.make_async_copy(share_hbm, share, in_sem.at[1]),
        pltpu.make_async_copy(rest_hbm, rest, in_sem.at[2]),
    ]
    for load in loads:
        load.start()

    barrier = pltpu.get_barrier_semaphore()
    for j in range(1, bands):
        pl.semaphore_signal(
            barrier, inc=1, device_id=(lax.rem(k + j, bands), m), device_id_type=MESH
        )

    @pl.when(m > 0)
    def _():
        for j in range(bands):
            pl.semaphore_signal(
                barrier, inc=1, device_id=(lax.rem(k + j, bands), m - 1), device_id_type=MESH
            )

    lane = lax.broadcasted_iota(jnp.int32, (SUBLANES, LANES), 1)
    base_rows[...] = jnp.zeros_like(base_rows)

    @pl.when(m == 0)
    def _():
        before[...] = jnp.zeros_like(before)

    for load in loads:
        load.wait()

    row_of = lax.broadcasted_iota(jnp.int32, (local, local * SUMMED), 0)
    channel = lax.broadcasted_iota(jnp.int32, (local, local * SUMMED), 1)
    ones = jnp.where(channel // SUMMED == row_of, 1.0, 0.0).astype(jnp.bfloat16)
    base = jnp.dot(ones, spec[...], preferred_element_type=jnp.float32)
    for q in range(chunks):
        base_rows[:, q, :] = base[:, q * LANES : (q + 1) * LANES]
    state = [[base_rows[s]] for s in range(local)]
    count = 2
    while count <= local:
        state = merged(state, count, 0, k * (local // count), all_trials, share, rest, lane)
        count = count * 2
    for d in range(local):
        rows[d] = state[0][d][: chunks + 1]

    @pl.when(m < slots - 1)
    def _():
        pl.semaphore_wait(barrier, 2 * bands - 1)

    @pl.when(m == slots - 1)
    def _():
        pl.semaphore_wait(barrier, bands - 1)

    def here_copy(j):
        to = lax.rem(k + j, bands)
        return pltpu.make_async_remote_copy(
            src_ref=rows.at[pl.ds(to * each, each)], dst_ref=here.at[k],
            send_sem=here_send.at[j], recv_sem=here_recv.at[j],
            device_id=(to, m), device_id_type=MESH,
        )

    def next_copy(j):
        to = lax.rem(k + j, bands)
        return pltpu.make_async_remote_copy(
            src_ref=rows.at[pl.ds(to * each, each)], dst_ref=before.at[k],
            send_sem=next_send.at[j], recv_sem=next_recv.at[j],
            device_id=(to, m + 1), device_id_type=MESH,
        )

    def arrival(buffer, sems, j):
        came = buffer.at[lax.rem(k + bands - j, bands)]
        return pltpu.make_async_remote_copy(
            src_ref=came, dst_ref=came, send_sem=sems.at[j], recv_sem=sems.at[j],
            device_id=(k, m), device_id_type=MESH,
        )

    order = sorted(range(bands), key=lambda j: -min(j, bands - j))

    @pl.when(m < slots - 1)
    def _():
        for j in order:
            next_copy(j).start()

    for j in order:
        if j > 0:
            here_copy(j).start()
    here[k] = rows[pl.ds(k * each, each)]

    for j in range(1, bands):
        arrival(here, here_recv, j).wait_recv()

    @pl.when(m > 0)
    def _():
        for j in range(bands):
            arrival(before, next_recv, j).wait_recv()

    state = []
    for s in range(bands):
        trials = []
        for i in range(each):
            own, old = here[s, i], before[s, i]
            joint = own[:1] + old[chunks:]
            trials.append(jnp.concatenate([old[:chunks], joint, own[1:chunks]], axis=0))
        state.append(trials)
    width = each
    while count <= all_trials:
        width = width * 2
        state = merged(state, count, k * width, 0, all_trials, share, rest, lane)
        count = count * 2

    window = state[0]
    flat = 0
    piece = part.shape[1]
    for level in range(WIDTHS):
        w = 2**level
        peak = functools.reduce(jnp.maximum, window)[chunks:]
        peak = peak * (1.0 / math.sqrt(all_trials * SUMMED * w))
        done = 0
        while done < chunks:
            slot = flat % piece
            take = min(chunks - done, piece - slot)
            part[flat // piece, slot : slot + take, :] = peak[done : done + take]
            done, flat = done + take, flat + take
        if level + 1 < WIDTHS:
            later = []
            for row in window:
                above = pltpu.roll(row, 1, 0)
                if w < LANES:
                    above = moved(row, above, w, lane)
                later.append(row + above)
            window = later
    while flat < bands * piece:
        part[flat // piece, flat % piece : flat % piece + 1, :] = jnp.zeros((1, LANES), jnp.float32)
        flat = flat + 1

    def part_copy(j):
        to = lax.rem(k + j, bands)
        return pltpu.make_async_remote_copy(
            src_ref=part.at[to], dst_ref=parts.at[k],
            send_sem=part_send.at[j], recv_sem=part_recv.at[j],
            device_id=(to, m), device_id_type=MESH,
        )

    def whole_copy(j):
        to = lax.rem(k + j, bands)
        return pltpu.make_async_remote_copy(
            src_ref=mine, dst_ref=whole.at[k],
            send_sem=all_send.at[j], recv_sem=all_recv.at[j],
            device_id=(to, m), device_id_type=MESH,
        )

    for j in order:
        if j > 0:
            part_copy(j).start()
    parts[k] = part[k]
    for j in range(1, bands):
        arrival(parts, part_recv, j).wait_recv()
    mine[...] = functools.reduce(jnp.maximum, [parts[s] for s in range(bands)])
    for j in order:
        if j > 0:
            whole_copy(j).start()
    whole[k] = mine[...]
    for j in range(1, bands):
        here_copy(j).wait_send()
        part_copy(j).wait_send()

    @pl.when(m < slots - 1)
    def _():
        for j in range(bands):
            next_copy(j).wait_send()

    for j in range(1, bands):
        arrival(whole, all_recv, j).wait_recv()
    for flat in range(WIDTHS * chunks):
        at = flat % chunks * LANES
        best_ref[flat // chunks : flat // chunks + 1, at : at + LANES] = whole[
            flat // piece, flat % piece : flat % piece + 1, :
        ]
    for j in range(1, bands):
        whole_copy(j).wait_send()


def one_block_back(mesh, channels, span, all_trials):
    bands = mesh.shape["freq"]
    local = channels // bands // SUMMED
    if span * 2 != SUBLANES * LANES or all_trials > LANES or local % bands != 0:
        return False
    reach = sum(2**level - 1 for level in range(1, all_trials.bit_length()))
    return reach + 2 ** (WIDTHS - 1) - 1 <= span


def shards_one_back(bands, slots, spectrogram, low_share, jitter):
    depth, span = spectrogram.shape
    all_trials = low_share.shape[0] + 1
    local = depth // SUMMED
    chunks = span // LANES
    each = local // bands
    piece = -(-WIDTHS * chunks // bands)
    sems = pltpu.SemaphoreType.DMA((bands,))
    vmem = lambda *shape: pltpu.VMEM(shape, jnp.float32)
    return pl.pallas_call(
        functools.partial(search, bands, slots, all_trials),
        out_shape=jax.ShapeDtypeStruct((WIDTHS, span), jnp.float32),
        in_specs=[pl.BlockSpec(memory_space=pl.ANY)] * 3,
        out_specs=pl.BlockSpec(memory_space=pltpu.VMEM),
        scratch_shapes=[
            pltpu.VMEM((depth, span), spectrogram.dtype),
            pltpu.SMEM(low_share.shape, jnp.int32),
            pltpu.SMEM(jitter.shape, jnp.int32),
            vmem(local, SUBLANES, LANES),
            vmem(local, chunks + 1, LANES),
            vmem(bands, each, chunks + 1, LANES),
            vmem(bands, each, chunks + 1, LANES),
            vmem(bands, piece, LANES),
            vmem(bands, piece, LANES),
            vmem(piece, LANES),
            vmem(bands, piece, LANES),
            pltpu.SemaphoreType.DMA((3,)),
        ]
        + [sems] * 8,
        compiler_params=pltpu.CompilerParams(
            collective_id=0, has_side_effects=True, vmem_limit_bytes=16 * 2**20
        ),
    )(spectrogram, low_share, jitter)


def solution(mesh):
    placed = (P("freq", "tm"), P(), P())
    bands, slots = mesh.shape["freq"], mesh.shape["tm"]

    def run(spectrogram, low_share, jitter):
        channels, time = spectrogram.shape
        body = shards_any_reach
        if one_block_back(mesh, channels, time // slots, low_share.shape[0] + 1):
            body = functools.partial(shards_one_back, bands, slots)
        return jax.shard_map(
            body, mesh=mesh, in_specs=placed, out_specs=P(None, "tm"), check_vma=False
        )(spectrogram, low_share, jitter)

    return run
```

```python
import functools
import math

import jax
import jax.numpy as jnp
from jax import lax
from jax.experimental import pallas as pl
from jax.experimental.pallas import tpu as pltpu
from jax.sharding import PartitionSpec as P

SUMMED = 32
WIDTHS = 9
LANES = 128
SUBLANES = 8
MESH = pl.DeviceIdType.MESH


def passed_along(block, axis, distance):
    devices = range(lax.axis_size(axis))
    route = [(i - distance, i) for i in devices if i - distance in devices]
    return lax.ppermute(block, axis, route)


def swapped(block, axis, apart):
    count = lax.axis_size(axis)
    route = []
    for low in range(count):
        high = low | 1 << apart
        if high != low and high < count:
            route += [(low, high), (high, low)]
    return lax.ppermute(block, axis, route)


def widen(trial_rows, fetch_width):
    if fetch_width == 0:
        return trial_rows
    span_time = trial_rows.shape[-1]
    hop_count = min(-(-fetch_width // span_time), lax.axis_size("tm") - 1)
    pieces = [trial_rows]
    fetched = 0
    for hop_index in range(1, hop_count + 1):
        taken_cols = min(span_time, fetch_width - fetched)
        arrived = passed_along(trial_rows[..., span_time - taken_cols :], "tm", hop_index)
        pieces.insert(0, arrived)
        fetched = fetched + taken_cols
    if fetched < fetch_width:
        pieces.insert(
            0, jnp.zeros(trial_rows.shape[:-1] + (fetch_width - fetched,), trial_rows.dtype)
        )
    return jnp.concatenate(pieces, axis=-1)


def align_pair(low_set, high_set, margin, need_now, fetch_width):
    if fetch_width == 0:
        return (low_set[..., need_now:], high_set, margin - need_now)
    high_set = widen(high_set, fetch_width)
    low_set = widen(low_set, fetch_width - need_now)
    return (low_set, high_set, fetch_width - need_now)


def delay_of(trial_ids, subband_ids, trial_count, low_share, jitter):
    all_trials = low_share.shape[0] + 1
    rate_rows = jnp.take(low_share, all_trials // trial_count - 1 + subband_ids)
    return (trial_ids * rate_rows + jnp.take(jitter, trial_count - 2 + trial_ids)) // 64


def merge_rows(low_rows, high_rows, shifts, need_now):
    offsets = need_now - shifts
    bit_count = max(need_now.bit_length(), 1)
    moved = high_rows
    for bit_index in range(bit_count):
        step_size = 2**bit_index
        cols = moved.shape[-1]
        selected = (offsets >> bit_index & 1)[:, None] == 1
        moved = jnp.where(selected, moved[:, step_size:], moved[:, : cols - step_size])
    return low_rows + moved


def shards_any_reach(spectrogram, low_share, jitter):
    trial_dev = spectrogram.shape[0] // SUMMED
    span_time = spectrogram.shape[1]
    all_trials = low_share.shape[0] + 1
    freq_bits = lax.axis_size("freq").bit_length() - 1
    device = lax.axis_index("freq")
    local_counts = []
    trial_count = 2
    while trial_count <= trial_dev:
        local_counts.append(trial_count)
        trial_count = trial_count * 2
    cross_counts = [trial_dev * 2 ** (bit_index + 1) for bit_index in range(freq_bits)]
    need_list = [count_now - 1 for count_now in local_counts + cross_counts] + [
        2 ** (WIDTHS - 1) - 1
    ]
    fetch_plan = []
    margin = 0
    for position in range(len(need_list)):
        need_now = need_list[position]
        if margin >= need_now:
            fetch_plan.append(0)
            margin = margin - need_now
            continue
        fetch_width = need_now
        for later_need in need_list[position + 1 :]:
            if fetch_width + later_need > span_time:
                break
            fetch_width = fetch_width + later_need
        fetch_plan.append(fetch_width)
        margin = fetch_width - need_now
    states = jnp.sum(spectrogram.reshape(trial_dev, SUMMED, span_time), axis=1, dtype=jnp.float32)[
        :, None, :
    ]
    margin = 0
    section_index = 0
    for trial_count in local_counts:
        need_now = trial_count - 1
        groups = states.shape[0] // 2
        low_set, high_set, margin = align_pair(
            states[0::2], states[1::2], margin, need_now, fetch_plan[section_index]
        )
        low_rows = jnp.repeat(low_set, 2, axis=1).reshape(groups * trial_count, -1)
        high_rows = jnp.repeat(high_set, 2, axis=1).reshape(groups * trial_count, -1)
        trial_ids = jnp.tile(jnp.arange(trial_count, dtype=jnp.int32), groups)
        subband_ids = device * (trial_dev // trial_count) + jnp.repeat(
            jnp.arange(groups, dtype=jnp.int32), trial_count
        )
        shifts = delay_of(trial_ids, subband_ids, trial_count, low_share, jitter)
        states = merge_rows(low_rows, high_rows, shifts, need_now).reshape(groups, trial_count, -1)
        section_index = section_index + 1
    trial_rows = states[0]
    trial_ids = jnp.arange(trial_dev, dtype=jnp.int32)
    for bit_index in range(freq_bits):
        trial_count = cross_counts[bit_index]
        need_now = trial_count - 1
        partner = swapped(trial_rows, "freq", bit_index)
        upper_half = device >> bit_index & 1
        low_rows = jnp.where(upper_half == 1, partner, trial_rows)
        high_rows = jnp.where(upper_half == 1, trial_rows, partner)
        low_rows, high_rows, margin = align_pair(
            low_rows, high_rows, margin, need_now, fetch_plan[section_index]
        )
        trial_ids = 2 * trial_ids + upper_half
        shifts = delay_of(trial_ids, device >> bit_index + 1, trial_count, low_share, jitter)
        trial_rows = merge_rows(low_rows, high_rows, shifts, need_now)
        section_index = section_index + 1
    if fetch_plan[section_index] > 0:
        trial_rows = widen(trial_rows, fetch_plan[section_index])
    signal = trial_rows / math.sqrt(all_trials * SUMMED)
    peak_rows = []
    window_sum = signal
    width_now = 1
    for level_index in range(WIDTHS):
        length = window_sum.shape[1]
        peak_rows.append(
            jnp.max(window_sum[:, length - span_time :], axis=0) / math.sqrt(width_now)
        )
        if level_index + 1 < WIDTHS:
            window_sum = window_sum[:, width_now:] + window_sum[:, : length - width_now]
            width_now = width_now * 2
    local_best = jnp.stack(peak_rows)
    return lax.pmax(local_best, "freq")


def moved(row, above, delay, lane):
    return pltpu.roll(jnp.where(lane >= LANES - delay, above, row), delay, 1)


def merged(old, count, first_trial, first_subband, all_trials, share, rest, lane):
    new = []
    for s in range(len(old) // 2):
        rate = share[all_trials // count - 1 + first_subband + s]
        highs = [(row, pltpu.roll(row, 1, 0)) for row in old[2 * s + 1]]
        trials = []
        for j in range(2 * len(highs)):
            trial = first_trial + j
            delay = (trial * rate + rest[count - 2 + trial]) >> 6
            trials.append(old[2 * s][j // 2] + moved(*highs[j // 2], delay, lane))
        new.append(trials)
    return new


def search(
    bands, slots, all_trials,
    spec_hbm, share_hbm, rest_hbm, best_ref,
    spec, share, rest, base_rows, rows, here, before, part, parts, mine, whole,
    in_sem, here_send, here_recv, next_send, next_recv, part_send, part_recv, all_send, all_recv,
):
    k, m = lax.axis_index("freq"), lax.axis_index("tm")
    span = spec.shape[1]
    chunks = span // LANES
    local = spec.shape[0] // SUMMED
    each = local // bands

    loads = [
        pltpu.make_async_copy(spec_hbm, spec, in_sem.at[0]),
        pltpu.make_async_copy(share_hbm, share, in_sem.at[1]),
        pltpu.make_async_copy(rest_hbm, rest, in_sem.at[2]),
    ]
    for load in loads:
        load.start()

    barrier = pltpu.get_barrier_semaphore()
    for j in range(1, bands):
        pl.semaphore_signal(
            barrier, inc=1, device_id=(lax.rem(k + j, bands), m), device_id_type=MESH
        )

    @pl.when(m > 0)
    def _():
        for j in range(bands):
            pl.semaphore_signal(
                barrier, inc=1, device_id=(lax.rem(k + j, bands), m - 1), device_id_type=MESH
            )

    lane = lax.broadcasted_iota(jnp.int32, (SUBLANES, LANES), 1)
    base_rows[...] = jnp.zeros_like(base_rows)

    @pl.when(m == 0)
    def _():
        before[...] = jnp.zeros_like(before)

    for load in loads:
        load.wait()

    row_of = lax.broadcasted_iota(jnp.int32, (local, local * SUMMED), 0)
    channel = lax.broadcasted_iota(jnp.int32, (local, local * SUMMED), 1)
    ones = jnp.where(channel // SUMMED == row_of, 1.0, 0.0).astype(jnp.bfloat16)
    base = jnp.dot(ones, spec[...], preferred_element_type=jnp.float32)
    for q in range(chunks):
        base_rows[:, q, :] = base[:, q * LANES : (q + 1) * LANES]
    state = [[base_rows[s]] for s in range(local)]
    count = 2
    while count <= local:
        state = merged(state, count, 0, k * (local // count), all_trials, share, rest, lane)
        count = count * 2
    for d in range(local):
        rows[d] = state[0][d][: chunks + 1]

    @pl.when(m < slots - 1)
    def _():
        pl.semaphore_wait(barrier, 2 * bands - 1)

    @pl.when(m == slots - 1)
    def _():
        pl.semaphore_wait(barrier, bands - 1)

    def here_copy(j):
        to = lax.rem(k + j, bands)
        return pltpu.make_async_remote_copy(
            src_ref=rows.at[pl.ds(to * each, each)], dst_ref=here.at[k],
            send_sem=here_send.at[j], recv_sem=here_recv.at[j],
            device_id=(to, m), device_id_type=MESH,
        )

    def next_copy(j):
        to = lax.rem(k + j, bands)
        return pltpu.make_async_remote_copy(
            src_ref=rows.at[pl.ds(to * each, each)], dst_ref=before.at[k],
            send_sem=next_send.at[j], recv_sem=next_recv.at[j],
            device_id=(to, m + 1), device_id_type=MESH,
        )

    def arrival(buffer, sems, j):
        came = buffer.at[lax.rem(k + bands - j, bands)]
        return pltpu.make_async_remote_copy(
            src_ref=came, dst_ref=came, send_sem=sems.at[j], recv_sem=sems.at[j],
            device_id=(k, m), device_id_type=MESH,
        )

    order = sorted(range(bands), key=lambda j: -min(j, bands - j))

    @pl.when(m < slots - 1)
    def _():
        for j in order:
            next_copy(j).start()

    for j in order:
        if j > 0:
            here_copy(j).start()
    here[k] = rows[pl.ds(k * each, each)]

    for j in range(1, bands):
        arrival(here, here_recv, j).wait_recv()

    @pl.when(m > 0)
    def _():
        for j in range(bands):
            arrival(before, next_recv, j).wait_recv()

    state = []
    for s in range(bands):
        trials = []
        for i in range(each):
            own, old = here[s, i], before[s, i]
            joint = own[:1] + old[chunks:]
            trials.append(jnp.concatenate([old[:chunks], joint, own[1:chunks]], axis=0))
        state.append(trials)
    width = each
    while count <= all_trials:
        width = width * 2
        state = merged(state, count, k * width, 0, all_trials, share, rest, lane)
        count = count * 2

    window = state[0]
    flat = 0
    piece = part.shape[1]
    for level in range(WIDTHS):
        w = 2**level
        peak = functools.reduce(jnp.maximum, window)[chunks:]
        peak = peak * (1.0 / math.sqrt(all_trials * SUMMED * w))
        done = 0
        while done < chunks:
            slot = flat % piece
            take = min(chunks - done, piece - slot)
            part[flat // piece, slot : slot + take, :] = peak[done : done + take]
            done, flat = done + take, flat + take
        if level + 1 < WIDTHS:
            later = []
            for row in window:
                above = pltpu.roll(row, 1, 0)
                if w < LANES:
                    above = moved(row, above, w, lane)
                later.append(row + above)
            window = later
    while flat < bands * piece:
        part[flat // piece, flat % piece : flat % piece + 1, :] = jnp.zeros((1, LANES), jnp.float32)
        flat = flat + 1

    def part_copy(j):
        to = lax.rem(k + j, bands)
        return pltpu.make_async_remote_copy(
            src_ref=part.at[to], dst_ref=parts.at[k],
            send_sem=part_send.at[j], recv_sem=part_recv.at[j],
            device_id=(to, m), device_id_type=MESH,
        )

    def whole_copy(j):
        to = lax.rem(k + j, bands)
        return pltpu.make_async_remote_copy(
            src_ref=mine, dst_ref=whole.at[k],
            send_sem=all_send.at[j], recv_sem=all_recv.at[j],
            device_id=(to, m), device_id_type=MESH,
        )

    for j in order:
        if j > 0:
            part_copy(j).start()
    parts[k] = part[k]
    for j in range(1, bands):
        arrival(parts, part_recv, j).wait_recv()
    mine[...] = functools.reduce(jnp.maximum, [parts[s] for s in range(bands)])
    for j in order:
        if j > 0:
            whole_copy(j).start()
    whole[k] = mine[...]
    for j in range(1, bands):
        here_copy(j).wait_send()
        part_copy(j).wait_send()

    @pl.when(m < slots - 1)
    def _():
        for j in range(bands):
            next_copy(j).wait_send()

    for j in range(1, bands):
        arrival(whole, all_recv, j).wait_recv()
    for flat in range(WIDTHS * chunks):
        at = flat % chunks * LANES
        best_ref[flat // chunks : flat // chunks + 1, at : at + LANES] = whole[
            flat // piece, flat % piece : flat % piece + 1, :
        ]
    for j in range(1, bands):
        whole_copy(j).wait_send()


def one_block_back(mesh, channels, span, all_trials):
    bands = mesh.shape["freq"]
    local = channels // bands // SUMMED
    if span * 2 != SUBLANES * LANES or all_trials > LANES or local % bands != 0:
        return False
    reach = sum(2**level - 1 for level in range(1, all_trials.bit_length()))
    return reach + 2 ** (WIDTHS - 1) - 1 <= span


def shards_one_back(bands, slots, spectrogram, low_share, jitter):
    depth, span = spectrogram.shape
    all_trials = low_share.shape[0] + 1
    local = depth // SUMMED
    chunks = span // LANES
    each = local // bands
    piece = -(-WIDTHS * chunks // bands)
    sems = pltpu.SemaphoreType.DMA((bands,))
    vmem = lambda *shape: pltpu.VMEM(shape, jnp.float32)
    return pl.pallas_call(
        functools.partial(search, bands, slots, all_trials),
        out_shape=jax.ShapeDtypeStruct((WIDTHS, span), jnp.float32),
        in_specs=[pl.BlockSpec(memory_space=pltpu.HBM)] * 3,
        out_specs=pl.BlockSpec(memory_space=pltpu.VMEM),
        scratch_shapes=[
            pltpu.VMEM((depth, span), spectrogram.dtype),
            pltpu.SMEM(low_share.shape, jnp.int32),
            pltpu.SMEM(jitter.shape, jnp.int32),
            vmem(local, SUBLANES, LANES),
            vmem(local, chunks + 1, LANES),
            vmem(bands, each, chunks + 1, LANES),
            vmem(bands, each, chunks + 1, LANES),
            vmem(bands, piece, LANES),
            vmem(bands, piece, LANES),
            vmem(piece, LANES),
            vmem(bands, piece, LANES),
            pltpu.SemaphoreType.DMA((3,)),
        ]
        + [sems] * 8,
        compiler_params=pltpu.CompilerParams(
            collective_id=0, has_side_effects=True, vmem_limit_bytes=16 * 2**20
        ),
    )(spectrogram, low_share, jitter)


def solution(mesh):
    placed = (P("freq", "tm"), P(), P())
    bands, slots = mesh.shape["freq"], mesh.shape["tm"]

    def run(spectrogram, low_share, jitter):
        channels, time = spectrogram.shape
        body = shards_any_reach
        if one_block_back(mesh, channels, time // slots, low_share.shape[0] + 1):
            body = functools.partial(shards_one_back, bands, slots)
        return jax.shard_map(
            body, mesh=mesh, in_specs=placed, out_specs=P(None, "tm"), check_vma=False
        )(spectrogram, low_share, jitter)

    return run
```

```python
import functools
import math

import jax
import jax.numpy as jnp
from jax import lax
from jax.experimental import pallas as pl
from jax.experimental.pallas import tpu as pltpu
from jax.sharding import PartitionSpec as P

SUMMED = 32
WIDTHS = 9
LANES = 128
SUBLANES = 8
MESH = pl.DeviceIdType.MESH


def passed_along(block, axis, distance):
    devices = range(lax.axis_size(axis))
    route = [(i - distance, i) for i in devices if i - distance in devices]
    return lax.ppermute(block, axis, route)


def swapped(block, axis, apart):
    count = lax.axis_size(axis)
    route = []
    for low in range(count):
        high = low | 1 << apart
        if high != low and high < count:
            route += [(low, high), (high, low)]
    return lax.ppermute(block, axis, route)


def widen(trial_rows, fetch_width):
    if fetch_width == 0:
        return trial_rows
    span_time = trial_rows.shape[-1]
    hop_count = min(-(-fetch_width // span_time), lax.axis_size("tm") - 1)
    pieces = [trial_rows]
    fetched = 0
    for hop_index in range(1, hop_count + 1):
        taken_cols = min(span_time, fetch_width - fetched)
        arrived = passed_along(trial_rows[..., span_time - taken_cols :], "tm", hop_index)
        pieces.insert(0, arrived)
        fetched = fetched + taken_cols
    if fetched < fetch_width:
        pieces.insert(
            0, jnp.zeros(trial_rows.shape[:-1] + (fetch_width - fetched,), trial_rows.dtype)
        )
    return jnp.concatenate(pieces, axis=-1)


def align_pair(low_set, high_set, margin, need_now, fetch_width):
    if fetch_width == 0:
        return (low_set[..., need_now:], high_set, margin - need_now)
    high_set = widen(high_set, fetch_width)
    low_set = widen(low_set, fetch_width - need_now)
    return (low_set, high_set, fetch_width - need_now)


def delay_of(trial_ids, subband_ids, trial_count, low_share, jitter):
    all_trials = low_share.shape[0] + 1
    rate_rows = jnp.take(low_share, all_trials // trial_count - 1 + subband_ids)
    return (trial_ids * rate_rows + jnp.take(jitter, trial_count - 2 + trial_ids)) // 64


def merge_rows(low_rows, high_rows, shifts, need_now):
    offsets = need_now - shifts
    bit_count = max(need_now.bit_length(), 1)
    moved = high_rows
    for bit_index in range(bit_count):
        step_size = 2**bit_index
        cols = moved.shape[-1]
        selected = (offsets >> bit_index & 1)[:, None] == 1
        moved = jnp.where(selected, moved[:, step_size:], moved[:, : cols - step_size])
    return low_rows + moved


def shards_any_reach(spectrogram, low_share, jitter):
    trial_dev = spectrogram.shape[0] // SUMMED
    span_time = spectrogram.shape[1]
    all_trials = low_share.shape[0] + 1
    freq_bits = lax.axis_size("freq").bit_length() - 1
    device = lax.axis_index("freq")
    local_counts = []
    trial_count = 2
    while trial_count <= trial_dev:
        local_counts.append(trial_count)
        trial_count = trial_count * 2
    cross_counts = [trial_dev * 2 ** (bit_index + 1) for bit_index in range(freq_bits)]
    need_list = [count_now - 1 for count_now in local_counts + cross_counts] + [
        2 ** (WIDTHS - 1) - 1
    ]
    fetch_plan = []
    margin = 0
    for position in range(len(need_list)):
        need_now = need_list[position]
        if margin >= need_now:
            fetch_plan.append(0)
            margin = margin - need_now
            continue
        fetch_width = need_now
        for later_need in need_list[position + 1 :]:
            if fetch_width + later_need > span_time:
                break
            fetch_width = fetch_width + later_need
        fetch_plan.append(fetch_width)
        margin = fetch_width - need_now
    states = jnp.sum(spectrogram.reshape(trial_dev, SUMMED, span_time), axis=1, dtype=jnp.float32)[
        :, None, :
    ]
    margin = 0
    section_index = 0
    for trial_count in local_counts:
        need_now = trial_count - 1
        groups = states.shape[0] // 2
        low_set, high_set, margin = align_pair(
            states[0::2], states[1::2], margin, need_now, fetch_plan[section_index]
        )
        low_rows = jnp.repeat(low_set, 2, axis=1).reshape(groups * trial_count, -1)
        high_rows = jnp.repeat(high_set, 2, axis=1).reshape(groups * trial_count, -1)
        trial_ids = jnp.tile(jnp.arange(trial_count, dtype=jnp.int32), groups)
        subband_ids = device * (trial_dev // trial_count) + jnp.repeat(
            jnp.arange(groups, dtype=jnp.int32), trial_count
        )
        shifts = delay_of(trial_ids, subband_ids, trial_count, low_share, jitter)
        states = merge_rows(low_rows, high_rows, shifts, need_now).reshape(groups, trial_count, -1)
        section_index = section_index + 1
    trial_rows = states[0]
    trial_ids = jnp.arange(trial_dev, dtype=jnp.int32)
    for bit_index in range(freq_bits):
        trial_count = cross_counts[bit_index]
        need_now = trial_count - 1
        partner = swapped(trial_rows, "freq", bit_index)
        upper_half = device >> bit_index & 1
        low_rows = jnp.where(upper_half == 1, partner, trial_rows)
        high_rows = jnp.where(upper_half == 1, trial_rows, partner)
        low_rows, high_rows, margin = align_pair(
            low_rows, high_rows, margin, need_now, fetch_plan[section_index]
        )
        trial_ids = 2 * trial_ids + upper_half
        shifts = delay_of(trial_ids, device >> bit_index + 1, trial_count, low_share, jitter)
        trial_rows = merge_rows(low_rows, high_rows, shifts, need_now)
        section_index = section_index + 1
    if fetch_plan[section_index] > 0:
        trial_rows = widen(trial_rows, fetch_plan[section_index])
    signal = trial_rows / math.sqrt(all_trials * SUMMED)
    peak_rows = []
    window_sum = signal
    width_now = 1
    for level_index in range(WIDTHS):
        length = window_sum.shape[1]
        peak_rows.append(
            jnp.max(window_sum[:, length - span_time :], axis=0) / math.sqrt(width_now)
        )
        if level_index + 1 < WIDTHS:
            window_sum = window_sum[:, width_now:] + window_sum[:, : length - width_now]
            width_now = width_now * 2
    local_best = jnp.stack(peak_rows)
    return lax.pmax(local_best, "freq")


def moved(row, above, delay, lane):
    return pltpu.roll(jnp.where(lane >= LANES - delay, above, row), delay, 1)


def merged(old, count, first_trial, first_subband, all_trials, share, rest, lane):
    new = []
    for s in range(len(old) // 2):
        rate = share[all_trials // count - 1 + first_subband + s]
        highs = [(row, pltpu.roll(row, 1, 0)) for row in old[2 * s + 1]]
        trials = []
        for j in range(2 * len(highs)):
            trial = first_trial + j
            delay = (trial * rate + rest[count - 2 + trial]) >> 6
            trials.append(old[2 * s][j // 2] + moved(*highs[j // 2], delay, lane))
        new.append(trials)
    return new


def search(
    bands, slots, all_trials,
    spec_hbm, share_hbm, rest_hbm, best_ref,
    spec, share, rest, base_rows, rows, here, before, part, parts, mine, whole,
    in_sem, here_send, here_recv, next_send, next_recv, part_send, part_recv, all_send, all_recv,
):
    k, m = lax.axis_index("freq"), lax.axis_index("tm")
    span = spec.shape[1]
    chunks = span // LANES
    local = spec.shape[0] // SUMMED
    each = local // bands

    loads = [
        pltpu.make_async_copy(spec_hbm, spec, in_sem.at[0]),
        pltpu.make_async_copy(share_hbm, share, in_sem.at[1]),
        pltpu.make_async_copy(rest_hbm, rest, in_sem.at[2]),
    ]
    for load in loads:
        load.start()

    barrier = pltpu.get_barrier_semaphore()
    for j in range(1, bands):
        pl.semaphore_signal(
            barrier, inc=1, device_id=(lax.rem(k + j, bands), m), device_id_type=MESH
        )

    @pl.when(m > 0)
    def _():
        for j in range(bands):
            pl.semaphore_signal(
                barrier, inc=1, device_id=(lax.rem(k + j, bands), m - 1), device_id_type=MESH
            )

    lane = lax.broadcasted_iota(jnp.int32, (SUBLANES, LANES), 1)
    base_rows[...] = jnp.zeros_like(base_rows)

    @pl.when(m == 0)
    def _():
        before[...] = jnp.zeros_like(before)

    for load in loads:
        load.wait()

    row_of = lax.broadcasted_iota(jnp.int32, (local, local * SUMMED), 0)
    channel = lax.broadcasted_iota(jnp.int32, (local, local * SUMMED), 1)
    ones = jnp.where(channel // SUMMED == row_of, 1.0, 0.0).astype(jnp.bfloat16)
    base = jnp.dot(ones, spec[...], preferred_element_type=jnp.float32)
    for q in range(chunks):
        base_rows[:, q, :] = base[:, q * LANES : (q + 1) * LANES]
    state = [[base_rows[s]] for s in range(local)]
    count = 2
    while count <= local:
        state = merged(state, count, 0, k * (local // count), all_trials, share, rest, lane)
        count = count * 2
    for d in range(local):
        rows[d] = state[0][d][: chunks + 1]

    @pl.when(m < slots - 1)
    def _():
        pl.semaphore_wait(barrier, 2 * bands - 1)

    @pl.when(m == slots - 1)
    def _():
        pl.semaphore_wait(barrier, bands - 1)

    def here_copy(j):
        to = lax.rem(k + j, bands)
        return pltpu.make_async_remote_copy(
            src_ref=rows.at[pl.ds(to * each, each)], dst_ref=here.at[k],
            send_sem=here_send.at[j], recv_sem=here_recv.at[j],
            device_id=(to, m), device_id_type=MESH,
        )

    def next_copy(j):
        to = lax.rem(k + j, bands)
        return pltpu.make_async_remote_copy(
            src_ref=rows.at[pl.ds(to * each, each)], dst_ref=before.at[k],
            send_sem=next_send.at[j], recv_sem=next_recv.at[j],
            device_id=(to, m + 1), device_id_type=MESH,
        )

    def arrival(buffer, sems, j):
        came = buffer.at[lax.rem(k + bands - j, bands)]
        return pltpu.make_async_remote_copy(
            src_ref=came, dst_ref=came, send_sem=sems.at[j], recv_sem=sems.at[j],
            device_id=(k, m), device_id_type=MESH,
        )

    order = sorted(range(bands), key=lambda j: -min(j, bands - j))

    @pl.when(m < slots - 1)
    def _():
        for j in order:
            next_copy(j).start()

    for j in order:
        if j > 0:
            here_copy(j).start()
    here[k] = rows[pl.ds(k * each, each)]

    for j in range(1, bands):
        arrival(here, here_recv, j).wait_recv()

    @pl.when(m > 0)
    def _():
        for j in range(bands):
            arrival(before, next_recv, j).wait_recv()

    state = []
    for s in range(bands):
        trials = []
        for i in range(each):
            own, old = here[s, i], before[s, i]
            joint = own[:1] + old[chunks:]
            trials.append(jnp.concatenate([old[:chunks], joint, own[1:chunks]], axis=0))
        state.append(trials)
    width = each
    while count <= all_trials:
        width = width * 2
        state = merged(state, count, k * width, 0, all_trials, share, rest, lane)
        count = count * 2

    window = state[0]
    flat = 0
    piece = part.shape[1]
    for level in range(WIDTHS):
        w = 2**level
        peak = functools.reduce(jnp.maximum, window)[chunks:]
        peak = peak * (1.0 / math.sqrt(all_trials * SUMMED * w))
        done = 0
        while done < chunks:
            slot = flat % piece
            take = min(chunks - done, piece - slot)
            part[flat // piece, slot : slot + take, :] = peak[done : done + take]
            done, flat = done + take, flat + take
        if level + 1 < WIDTHS:
            later = []
            for row in window:
                above = pltpu.roll(row, 1, 0)
                if w < LANES:
                    above = moved(row, above, w, lane)
                later.append(row + above)
            window = later
    while flat < bands * piece:
        part[flat // piece, flat % piece : flat % piece + 1, :] = jnp.zeros((1, LANES), jnp.float32)
        flat = flat + 1

    def part_copy(j):
        to = lax.rem(k + j, bands)
        return pltpu.make_async_remote_copy(
            src_ref=part.at[to], dst_ref=parts.at[k],
            send_sem=part_send.at[j], recv_sem=part_recv.at[j],
            device_id=(to, m), device_id_type=MESH,
        )

    def whole_copy(j):
        to = lax.rem(k + j, bands)
        return pltpu.make_async_remote_copy(
            src_ref=mine, dst_ref=whole.at[k],
            send_sem=all_send.at[j], recv_sem=all_recv.at[j],
            device_id=(to, m), device_id_type=MESH,
        )

    for j in order:
        if j > 0:
            part_copy(j).start()
    parts[k] = part[k]
    for j in range(1, bands):
        arrival(parts, part_recv, j).wait_recv()
    mine[...] = functools.reduce(jnp.maximum, [parts[s] for s in range(bands)])
    for j in order:
        if j > 0:
            whole_copy(j).start()
    whole[k] = mine[...]
    for j in range(1, bands):
        here_copy(j).wait_send()
        part_copy(j).wait_send()

    @pl.when(m < slots - 1)
    def _():
        for j in range(bands):
            next_copy(j).wait_send()

    for j in range(1, bands):
        arrival(whole, all_recv, j).wait_recv()
    for flat in range(WIDTHS * chunks):
        at = flat % chunks * LANES
        best_ref[flat // chunks : flat // chunks + 1, at : at + LANES] = whole[
            flat // piece, flat % piece : flat % piece + 1, :
        ]
    for j in range(1, bands):
        whole_copy(j).wait_send()


def one_block_back(mesh, channels, span, all_trials):
    bands = mesh.shape["freq"]
    local = channels // bands // SUMMED
    if span * 2 != SUBLANES * LANES or all_trials > LANES or local % bands != 0:
        return False
    reach = sum(2**level - 1 for level in range(1, all_trials.bit_length()))
    return reach + 2 ** (WIDTHS - 1) - 1 <= span


def shards_one_back(bands, slots, spectrogram, low_share, jitter):
    depth, span = spectrogram.shape
    all_trials = low_share.shape[0] + 1
    local = depth // SUMMED
    chunks = span // LANES
    each = local // bands
    piece = -(-WIDTHS * chunks // bands)
    sems = pltpu.SemaphoreType.DMA((bands,))
    vmem = lambda *shape: pltpu.VMEM(shape, jnp.float32)
    return pl.pallas_call(
        functools.partial(search, bands, slots, all_trials),
        out_shape=jax.ShapeDtypeStruct((WIDTHS, span), jnp.float32),
        in_specs=[pl.BlockSpec(memory_space=pltpu.HBM)] * 3,
        out_specs=pl.BlockSpec(memory_space=pltpu.VMEM),
        scratch_shapes=[
            pltpu.VMEM((depth, span), spectrogram.dtype),
            pltpu.SMEM(low_share.shape, jnp.int32),
            pltpu.SMEM(jitter.shape, jnp.int32),
            vmem(local, SUBLANES, LANES),
            vmem(local, chunks + 1, LANES),
            vmem(bands, each, chunks + 1, LANES),
            vmem(bands, each, chunks + 1, LANES),
            vmem(bands, piece, LANES),
            vmem(bands, piece, LANES),
            vmem(piece, LANES),
            vmem(bands, piece, LANES),
            pltpu.SemaphoreType.DMA((3,)),
        ]
        + [sems] * 8,
        compiler_params=pltpu.CompilerParams(collective_id=0, has_side_effects=True),
    )(spectrogram, low_share, jitter)


def solution(mesh):
    placed = (P("freq", "tm"), P(), P())
    bands, slots = mesh.shape["freq"], mesh.shape["tm"]

    def run(spectrogram, low_share, jitter):
        channels, time = spectrogram.shape
        body = shards_any_reach
        if one_block_back(mesh, channels, time // slots, low_share.shape[0] + 1):
            body = functools.partial(shards_one_back, bands, slots)
        return jax.shard_map(
            body, mesh=mesh, in_specs=placed, out_specs=P(None, "tm"), check_vma=False
        )(spectrogram, low_share, jitter)

    return run
```

```python
import functools
import math

import jax
import jax.numpy as jnp
from jax import lax
from jax.experimental import pallas as pl
from jax.experimental.pallas import tpu as pltpu
from jax.sharding import PartitionSpec as P

SUMMED = 32
WIDTHS = 9
LANES = 128
SUBLANES = 8
MESH = pl.DeviceIdType.MESH


def passed_along(block, axis, distance):
    devices = range(lax.axis_size(axis))
    route = [(i - distance, i) for i in devices if i - distance in devices]
    return lax.ppermute(block, axis, route)


def swapped(block, axis, apart):
    count = lax.axis_size(axis)
    route = []
    for low in range(count):
        high = low | 1 << apart
        if high != low and high < count:
            route += [(low, high), (high, low)]
    return lax.ppermute(block, axis, route)


def widen(trial_rows, fetch_width):
    if fetch_width == 0:
        return trial_rows
    span_time = trial_rows.shape[-1]
    hop_count = min(-(-fetch_width // span_time), lax.axis_size("tm") - 1)
    pieces = [trial_rows]
    fetched = 0
    for hop_index in range(1, hop_count + 1):
        taken_cols = min(span_time, fetch_width - fetched)
        arrived = passed_along(trial_rows[..., span_time - taken_cols :], "tm", hop_index)
        pieces.insert(0, arrived)
        fetched = fetched + taken_cols
    if fetched < fetch_width:
        pieces.insert(
            0, jnp.zeros(trial_rows.shape[:-1] + (fetch_width - fetched,), trial_rows.dtype)
        )
    return jnp.concatenate(pieces, axis=-1)


def align_pair(low_set, high_set, margin, need_now, fetch_width):
    if fetch_width == 0:
        return (low_set[..., need_now:], high_set, margin - need_now)
    high_set = widen(high_set, fetch_width)
    low_set = widen(low_set, fetch_width - need_now)
    return (low_set, high_set, fetch_width - need_now)


def delay_of(trial_ids, subband_ids, trial_count, low_share, jitter):
    all_trials = low_share.shape[0] + 1
    rate_rows = jnp.take(low_share, all_trials // trial_count - 1 + subband_ids)
    return (trial_ids * rate_rows + jnp.take(jitter, trial_count - 2 + trial_ids)) // 64


def merge_rows(low_rows, high_rows, shifts, need_now):
    offsets = need_now - shifts
    bit_count = max(need_now.bit_length(), 1)
    moved = high_rows
    for bit_index in range(bit_count):
        step_size = 2**bit_index
        cols = moved.shape[-1]
        selected = (offsets >> bit_index & 1)[:, None] == 1
        moved = jnp.where(selected, moved[:, step_size:], moved[:, : cols - step_size])
    return low_rows + moved


def shards_any_reach(spectrogram, low_share, jitter):
    trial_dev = spectrogram.shape[0] // SUMMED
    span_time = spectrogram.shape[1]
    all_trials = low_share.shape[0] + 1
    freq_bits = lax.axis_size("freq").bit_length() - 1
    device = lax.axis_index("freq")
    local_counts = []
    trial_count = 2
    while trial_count <= trial_dev:
        local_counts.append(trial_count)
        trial_count = trial_count * 2
    cross_counts = [trial_dev * 2 ** (bit_index + 1) for bit_index in range(freq_bits)]
    need_list = [count_now - 1 for count_now in local_counts + cross_counts] + [
        2 ** (WIDTHS - 1) - 1
    ]
    fetch_plan = []
    margin = 0
    for position in range(len(need_list)):
        need_now = need_list[position]
        if margin >= need_now:
            fetch_plan.append(0)
            margin = margin - need_now
            continue
        fetch_width = need_now
        for later_need in need_list[position + 1 :]:
            if fetch_width + later_need > span_time:
                break
            fetch_width = fetch_width + later_need
        fetch_plan.append(fetch_width)
        margin = fetch_width - need_now
    states = jnp.sum(spectrogram.reshape(trial_dev, SUMMED, span_time), axis=1, dtype=jnp.float32)[
        :, None, :
    ]
    margin = 0
    section_index = 0
    for trial_count in local_counts:
        need_now = trial_count - 1
        groups = states.shape[0] // 2
        low_set, high_set, margin = align_pair(
            states[0::2], states[1::2], margin, need_now, fetch_plan[section_index]
        )
        low_rows = jnp.repeat(low_set, 2, axis=1).reshape(groups * trial_count, -1)
        high_rows = jnp.repeat(high_set, 2, axis=1).reshape(groups * trial_count, -1)
        trial_ids = jnp.tile(jnp.arange(trial_count, dtype=jnp.int32), groups)
        subband_ids = device * (trial_dev // trial_count) + jnp.repeat(
            jnp.arange(groups, dtype=jnp.int32), trial_count
        )
        shifts = delay_of(trial_ids, subband_ids, trial_count, low_share, jitter)
        states = merge_rows(low_rows, high_rows, shifts, need_now).reshape(groups, trial_count, -1)
        section_index = section_index + 1
    trial_rows = states[0]
    trial_ids = jnp.arange(trial_dev, dtype=jnp.int32)
    for bit_index in range(freq_bits):
        trial_count = cross_counts[bit_index]
        need_now = trial_count - 1
        partner = swapped(trial_rows, "freq", bit_index)
        upper_half = device >> bit_index & 1
        low_rows = jnp.where(upper_half == 1, partner, trial_rows)
        high_rows = jnp.where(upper_half == 1, trial_rows, partner)
        low_rows, high_rows, margin = align_pair(
            low_rows, high_rows, margin, need_now, fetch_plan[section_index]
        )
        trial_ids = 2 * trial_ids + upper_half
        shifts = delay_of(trial_ids, device >> bit_index + 1, trial_count, low_share, jitter)
        trial_rows = merge_rows(low_rows, high_rows, shifts, need_now)
        section_index = section_index + 1
    if fetch_plan[section_index] > 0:
        trial_rows = widen(trial_rows, fetch_plan[section_index])
    signal = trial_rows / math.sqrt(all_trials * SUMMED)
    peak_rows = []
    window_sum = signal
    width_now = 1
    for level_index in range(WIDTHS):
        length = window_sum.shape[1]
        peak_rows.append(
            jnp.max(window_sum[:, length - span_time :], axis=0) / math.sqrt(width_now)
        )
        if level_index + 1 < WIDTHS:
            window_sum = window_sum[:, width_now:] + window_sum[:, : length - width_now]
            width_now = width_now * 2
    local_best = jnp.stack(peak_rows)
    return lax.pmax(local_best, "freq")


def moved(row, above, delay, lane):
    return pltpu.roll(jnp.where(lane >= LANES - delay, above, row), delay, 1)


def merged(old, count, first_trial, first_subband, all_trials, share, rest, lane):
    new = []
    for s in range(len(old) // 2):
        rate = share[all_trials // count - 1 + first_subband + s]
        highs = [(row, pltpu.roll(row, 1, 0)) for row in old[2 * s + 1]]
        trials = []
        for j in range(2 * len(highs)):
            trial = first_trial + j
            delay = (trial * rate + rest[count - 2 + trial]) >> 6
            trials.append(old[2 * s][j // 2] + moved(*highs[j // 2], delay, lane))
        new.append(trials)
    return new


def search(
    bands, slots, all_trials, cuts,
    spec_hbm, share_hbm, rest_hbm, best_ref,
    spec, share, rest, base_rows, rows, here, before, part, parts,
    in_sem, here_send, here_recv, next_send, next_recv, part_send, part_recv,
):
    k, m = lax.axis_index("freq"), lax.axis_index("tm")
    span = spec.shape[1]
    chunks = span // LANES
    local = spec.shape[0] // SUMMED
    each = local // bands

    loads = [
        pltpu.make_async_copy(spec_hbm, spec, in_sem.at[0]),
        pltpu.make_async_copy(share_hbm, share, in_sem.at[1]),
        pltpu.make_async_copy(rest_hbm, rest, in_sem.at[2]),
    ]
    for load in loads:
        load.start()

    barrier = pltpu.get_barrier_semaphore()
    for j in range(1, bands):
        pl.semaphore_signal(
            barrier, inc=1, device_id=(lax.rem(k + j, bands), m), device_id_type=MESH
        )

    @pl.when(m > 0)
    def _():
        for j in range(bands):
            pl.semaphore_signal(
                barrier, inc=1, device_id=(lax.rem(k + j, bands), m - 1), device_id_type=MESH
            )

    lane = lax.broadcasted_iota(jnp.int32, (SUBLANES, LANES), 1)
    base_rows[...] = jnp.zeros_like(base_rows)

    @pl.when(m == 0)
    def _():
        before[...] = jnp.zeros_like(before)

    for load in loads:
        load.wait()

    row_of = lax.broadcasted_iota(jnp.int32, (local, local * SUMMED), 0)
    channel = lax.broadcasted_iota(jnp.int32, (local, local * SUMMED), 1)
    ones = jnp.where(channel // SUMMED == row_of, 1.0, 0.0).astype(jnp.bfloat16)
    base = jnp.dot(ones, spec[...], preferred_element_type=jnp.float32)
    for q in range(chunks):
        base_rows[:, q, :] = base[:, q * LANES : (q + 1) * LANES]
    state = [[base_rows[s]] for s in range(local)]
    count = 2
    while count <= local:
        state = merged(state, count, 0, k * (local // count), all_trials, share, rest, lane)
        count = count * 2
    for d in range(local):
        rows[d] = state[0][d][: chunks + 1]

    @pl.when(m < slots - 1)
    def _():
        pl.semaphore_wait(barrier, 2 * bands - 1)

    @pl.when(m == slots - 1)
    def _():
        pl.semaphore_wait(barrier, bands - 1)

    def here_copy(j):
        to = lax.rem(k + j, bands)
        return pltpu.make_async_remote_copy(
            src_ref=rows.at[pl.ds(to * each, each)], dst_ref=here.at[k],
            send_sem=here_send.at[j], recv_sem=here_recv.at[j],
            device_id=(to, m), device_id_type=MESH,
        )

    def next_copy(j):
        to = lax.rem(k + j, bands)
        return pltpu.make_async_remote_copy(
            src_ref=rows.at[pl.ds(to * each, each)], dst_ref=before.at[k],
            send_sem=next_send.at[j], recv_sem=next_recv.at[j],
            device_id=(to, m + 1), device_id_type=MESH,
        )

    def arrival(buffer, sems, j):
        came = buffer.at[lax.rem(k + bands - j, bands)]
        return pltpu.make_async_remote_copy(
            src_ref=came, dst_ref=came, send_sem=sems.at[j], recv_sem=sems.at[j],
            device_id=(k, m), device_id_type=MESH,
        )

    order = sorted(range(bands), key=lambda j: -min(j, bands - j))

    @pl.when(m < slots - 1)
    def _():
        for j in order:
            next_copy(j).start()

    for j in order:
        if j > 0:
            here_copy(j).start()
    here[k] = rows[pl.ds(k * each, each)]

    for j in range(1, bands):
        arrival(here, here_recv, j).wait_recv()

    @pl.when(m > 0)
    def _():
        for j in range(bands):
            arrival(before, next_recv, j).wait_recv()

    state = []
    for s in range(bands):
        trials = []
        for i in range(each):
            own, old = here[s, i], before[s, i]
            joint = own[:1] + old[chunks:]
            trials.append(jnp.concatenate([old[:chunks], joint, own[1:chunks]], axis=0))
        state.append(trials)
    width = each
    while count <= all_trials:
        width = width * 2
        state = merged(state, count, k * width, 0, all_trials, share, rest, lane)
        count = count * 2

    def part_copy(j, i):
        span_rows = pl.ds(cuts[i], cuts[i + 1] - cuts[i])
        return pltpu.make_async_remote_copy(
            src_ref=part.at[span_rows], dst_ref=parts.at[k, span_rows],
            send_sem=part_send.at[i, j], recv_sem=part_recv.at[i, j],
            device_id=(lax.rem(k + j, bands), m), device_id_type=MESH,
        )

    def part_arrival(j, i):
        came = parts.at[lax.rem(k + bands - j, bands), pl.ds(cuts[i], cuts[i + 1] - cuts[i])]
        return pltpu.make_async_remote_copy(
            src_ref=came, dst_ref=came, send_sem=part_send.at[i, j], recv_sem=part_recv.at[i, j],
            device_id=(k, m), device_id_type=MESH,
        )

    window = state[0]
    sent = 0
    used = WIDTHS * chunks
    part[used:] = jnp.zeros((part.shape[0] - used, LANES), jnp.float32)
    for level in range(WIDTHS):
        w = 2**level
        peak = functools.reduce(jnp.maximum, window)[chunks:]
        part[level * chunks : (level + 1) * chunks] = peak * (
            1.0 / math.sqrt(all_trials * SUMMED * w)
        )
        if (level + 1) * chunks == cuts[sent + 1] or level + 1 == WIDTHS:
            for j in order:
                if j > 0:
                    part_copy(j, sent).start()
            sent = sent + 1
        if level + 1 < WIDTHS:
            later = []
            for row in window:
                above = pltpu.roll(row, 1, 0)
                if w < LANES:
                    above = moved(row, above, w, lane)
                later.append(row + above)
            window = later
    for j in range(1, bands):
        here_copy(j).wait_send()

    @pl.when(m < slots - 1)
    def _():
        for j in range(bands):
            next_copy(j).wait_send()

    parts[k] = part[...]
    for i in range(len(cuts) - 1):
        for j in range(1, bands):
            part_arrival(j, i).wait_recv()
        best = functools.reduce(
            jnp.maximum, [parts[s, cuts[i] : cuts[i + 1]] for s in range(bands)]
        )
        for flat in range(cuts[i], min(cuts[i + 1], used)):
            at = flat % chunks * LANES
            best_ref[flat // chunks : flat // chunks + 1, at : at + LANES] = best[
                flat - cuts[i] : flat - cuts[i] + 1
            ]
    for i in range(len(cuts) - 1):
        for j in range(1, bands):
            part_copy(j, i).wait_send()


def one_block_back(mesh, channels, span, all_trials):
    bands = mesh.shape["freq"]
    local = channels // bands // SUMMED
    if span * 2 != SUBLANES * LANES or all_trials > LANES or local % bands != 0:
        return False
    reach = sum(2**level - 1 for level in range(1, all_trials.bit_length()))
    return reach + 2 ** (WIDTHS - 1) - 1 <= span


def shards_one_back(bands, slots, spectrogram, low_share, jitter):
    depth, span = spectrogram.shape
    all_trials = low_share.shape[0] + 1
    local = depth // SUMMED
    chunks = span // LANES
    each = local // bands
    cuts = (0, 16, -(-WIDTHS * chunks // SUBLANES) * SUBLANES)
    sems = pltpu.SemaphoreType.DMA((bands,))
    vmem = lambda *shape: pltpu.VMEM(shape, jnp.float32)
    return pl.pallas_call(
        functools.partial(search, bands, slots, all_trials, cuts),
        out_shape=jax.ShapeDtypeStruct((WIDTHS, span), jnp.float32),
        in_specs=[pl.BlockSpec(memory_space=pltpu.HBM)] * 3,
        out_specs=pl.BlockSpec(memory_space=pltpu.VMEM),
        scratch_shapes=[
            pltpu.VMEM((depth, span), spectrogram.dtype),
            pltpu.SMEM(low_share.shape, jnp.int32),
            pltpu.SMEM(jitter.shape, jnp.int32),
            vmem(local, SUBLANES, LANES),
            vmem(local, chunks + 1, LANES),
            vmem(bands, each, chunks + 1, LANES),
            vmem(bands, each, chunks + 1, LANES),
            vmem(cuts[-1], LANES),
            vmem(bands, cuts[-1], LANES),
            pltpu.SemaphoreType.DMA((3,)),
        ]
        + [sems] * 4
        + [pltpu.SemaphoreType.DMA((len(cuts) - 1, bands))] * 2,
        compiler_params=pltpu.CompilerParams(collective_id=0, has_side_effects=True),
    )(spectrogram, low_share, jitter)


def solution(mesh):
    placed = (P("freq", "tm"), P(), P())
    bands, slots = mesh.shape["freq"], mesh.shape["tm"]

    def run(spectrogram, low_share, jitter):
        channels, time = spectrogram.shape
        body = shards_any_reach
        if one_block_back(mesh, channels, time // slots, low_share.shape[0] + 1):
            body = functools.partial(shards_one_back, bands, slots)
        return jax.shard_map(
            body, mesh=mesh, in_specs=placed, out_specs=P(None, "tm"), check_vma=False
        )(spectrogram, low_share, jitter)

    return run
```

```python
import functools
import math

import jax
import jax.numpy as jnp
from jax import lax
from jax.experimental import pallas as pl
from jax.experimental.pallas import tpu as pltpu
from jax.sharding import PartitionSpec as P

SUMMED = 32
WIDTHS = 9
LANES = 128
SUBLANES = 8
MESH = pl.DeviceIdType.MESH


def passed_along(block, axis, distance):
    devices = range(lax.axis_size(axis))
    route = [(i - distance, i) for i in devices if i - distance in devices]
    return lax.ppermute(block, axis, route)


def swapped(block, axis, apart):
    count = lax.axis_size(axis)
    route = []
    for low in range(count):
        high = low | 1 << apart
        if high != low and high < count:
            route += [(low, high), (high, low)]
    return lax.ppermute(block, axis, route)


def widen(trial_rows, fetch_width):
    if fetch_width == 0:
        return trial_rows
    span_time = trial_rows.shape[-1]
    hop_count = min(-(-fetch_width // span_time), lax.axis_size("tm") - 1)
    pieces = [trial_rows]
    fetched = 0
    for hop_index in range(1, hop_count + 1):
        taken_cols = min(span_time, fetch_width - fetched)
        arrived = passed_along(trial_rows[..., span_time - taken_cols :], "tm", hop_index)
        pieces.insert(0, arrived)
        fetched = fetched + taken_cols
    if fetched < fetch_width:
        pieces.insert(
            0, jnp.zeros(trial_rows.shape[:-1] + (fetch_width - fetched,), trial_rows.dtype)
        )
    return jnp.concatenate(pieces, axis=-1)


def align_pair(low_set, high_set, margin, need_now, fetch_width):
    if fetch_width == 0:
        return (low_set[..., need_now:], high_set, margin - need_now)
    high_set = widen(high_set, fetch_width)
    low_set = widen(low_set, fetch_width - need_now)
    return (low_set, high_set, fetch_width - need_now)


def delay_of(trial_ids, subband_ids, trial_count, low_share, jitter):
    all_trials = low_share.shape[0] + 1
    rate_rows = jnp.take(low_share, all_trials // trial_count - 1 + subband_ids)
    return (trial_ids * rate_rows + jnp.take(jitter, trial_count - 2 + trial_ids)) // 64


def merge_rows(low_rows, high_rows, shifts, need_now):
    offsets = need_now - shifts
    bit_count = max(need_now.bit_length(), 1)
    moved = high_rows
    for bit_index in range(bit_count):
        step_size = 2**bit_index
        cols = moved.shape[-1]
        selected = (offsets >> bit_index & 1)[:, None] == 1
        moved = jnp.where(selected, moved[:, step_size:], moved[:, : cols - step_size])
    return low_rows + moved


def shards_any_reach(spectrogram, low_share, jitter):
    trial_dev = spectrogram.shape[0] // SUMMED
    span_time = spectrogram.shape[1]
    all_trials = low_share.shape[0] + 1
    freq_bits = lax.axis_size("freq").bit_length() - 1
    device = lax.axis_index("freq")
    local_counts = []
    trial_count = 2
    while trial_count <= trial_dev:
        local_counts.append(trial_count)
        trial_count = trial_count * 2
    cross_counts = [trial_dev * 2 ** (bit_index + 1) for bit_index in range(freq_bits)]
    need_list = [count_now - 1 for count_now in local_counts + cross_counts] + [
        2 ** (WIDTHS - 1) - 1
    ]
    fetch_plan = []
    margin = 0
    for position in range(len(need_list)):
        need_now = need_list[position]
        if margin >= need_now:
            fetch_plan.append(0)
            margin = margin - need_now
            continue
        fetch_width = need_now
        for later_need in need_list[position + 1 :]:
            if fetch_width + later_need > span_time:
                break
            fetch_width = fetch_width + later_need
        fetch_plan.append(fetch_width)
        margin = fetch_width - need_now
    states = jnp.sum(spectrogram.reshape(trial_dev, SUMMED, span_time), axis=1, dtype=jnp.float32)[
        :, None, :
    ]
    margin = 0
    section_index = 0
    for trial_count in local_counts:
        need_now = trial_count - 1
        groups = states.shape[0] // 2
        low_set, high_set, margin = align_pair(
            states[0::2], states[1::2], margin, need_now, fetch_plan[section_index]
        )
        low_rows = jnp.repeat(low_set, 2, axis=1).reshape(groups * trial_count, -1)
        high_rows = jnp.repeat(high_set, 2, axis=1).reshape(groups * trial_count, -1)
        trial_ids = jnp.tile(jnp.arange(trial_count, dtype=jnp.int32), groups)
        subband_ids = device * (trial_dev // trial_count) + jnp.repeat(
            jnp.arange(groups, dtype=jnp.int32), trial_count
        )
        shifts = delay_of(trial_ids, subband_ids, trial_count, low_share, jitter)
        states = merge_rows(low_rows, high_rows, shifts, need_now).reshape(groups, trial_count, -1)
        section_index = section_index + 1
    trial_rows = states[0]
    trial_ids = jnp.arange(trial_dev, dtype=jnp.int32)
    for bit_index in range(freq_bits):
        trial_count = cross_counts[bit_index]
        need_now = trial_count - 1
        partner = swapped(trial_rows, "freq", bit_index)
        upper_half = device >> bit_index & 1
        low_rows = jnp.where(upper_half == 1, partner, trial_rows)
        high_rows = jnp.where(upper_half == 1, trial_rows, partner)
        low_rows, high_rows, margin = align_pair(
            low_rows, high_rows, margin, need_now, fetch_plan[section_index]
        )
        trial_ids = 2 * trial_ids + upper_half
        shifts = delay_of(trial_ids, device >> bit_index + 1, trial_count, low_share, jitter)
        trial_rows = merge_rows(low_rows, high_rows, shifts, need_now)
        section_index = section_index + 1
    if fetch_plan[section_index] > 0:
        trial_rows = widen(trial_rows, fetch_plan[section_index])
    signal = trial_rows / math.sqrt(all_trials * SUMMED)
    peak_rows = []
    window_sum = signal
    width_now = 1
    for level_index in range(WIDTHS):
        length = window_sum.shape[1]
        peak_rows.append(
            jnp.max(window_sum[:, length - span_time :], axis=0) / math.sqrt(width_now)
        )
        if level_index + 1 < WIDTHS:
            window_sum = window_sum[:, width_now:] + window_sum[:, : length - width_now]
            width_now = width_now * 2
    local_best = jnp.stack(peak_rows)
    return lax.pmax(local_best, "freq")


def moved(row, above, delay, lane):
    return pltpu.roll(jnp.where(lane >= LANES - delay, above, row), delay, 1)


def merged(old, count, first_trial, first_subband, all_trials, share, rest, lane):
    new = []
    for s in range(len(old) // 2):
        rate = share[all_trials // count - 1 + first_subband + s]
        highs = [(row, pltpu.roll(row, 1, 0)) for row in old[2 * s + 1]]
        trials = []
        for j in range(2 * len(highs)):
            trial = first_trial + j
            delay = (trial * rate + rest[count - 2 + trial]) >> 6
            trials.append(old[2 * s][j // 2] + moved(*highs[j // 2], delay, lane))
        new.append(trials)
    return new


def search(
    bands, slots, all_trials, cuts,
    spec_hbm, share_hbm, rest_hbm, best_ref,
    spec, share, rest, base_rows, rows, here, before, part, parts,
    in_sem, sems, part_sems,
):
    k, m = lax.axis_index("freq"), lax.axis_index("tm")
    span = spec.shape[1]
    chunks = span // LANES
    local = spec.shape[0] // SUMMED
    each = local // bands

    half = local // 2
    spec_loads = []
    for i in range(2):
        channels = pl.ds(i * half * SUMMED, half * SUMMED)
        spec_loads.append(
            pltpu.make_async_copy(spec_hbm.at[channels], spec.at[channels], in_sem.at[i])
        )
    table_loads = [
        pltpu.make_async_copy(share_hbm, share, in_sem.at[2]),
        pltpu.make_async_copy(rest_hbm, rest, in_sem.at[3]),
    ]
    for load in spec_loads + table_loads:
        load.start()

    barrier = pltpu.get_barrier_semaphore()
    for j in range(1, bands):
        pl.semaphore_signal(
            barrier, inc=1, device_id=(lax.rem(k + j, bands), m), device_id_type=MESH
        )

    @pl.when(m > 0)
    def _():
        for j in range(bands):
            pl.semaphore_signal(
                barrier, inc=1, device_id=(lax.rem(k + j, bands), m - 1), device_id_type=MESH
            )

    lane = lax.broadcasted_iota(jnp.int32, (SUBLANES, LANES), 1)
    base_rows[...] = jnp.zeros_like(base_rows)

    @pl.when(m == 0)
    def _():
        before[...] = jnp.zeros_like(before)

    row_of = lax.broadcasted_iota(jnp.int32, (half, half * SUMMED), 0)
    channel = lax.broadcasted_iota(jnp.int32, (half, half * SUMMED), 1)
    ones = jnp.where(channel // SUMMED == row_of, 1.0, 0.0).astype(jnp.bfloat16)
    for i in range(2):
        spec_loads[i].wait()
        base = jnp.dot(
            ones,
            spec[i * half * SUMMED : (i + 1) * half * SUMMED],
            preferred_element_type=jnp.float32,
        )
        for q in range(chunks):
            base_rows[i * half : (i + 1) * half, q, :] = base[:, q * LANES : (q + 1) * LANES]
    for load in table_loads:
        load.wait()
    state = [[base_rows[s]] for s in range(local)]
    count = 2
    while count <= local:
        state = merged(state, count, 0, k * (local // count), all_trials, share, rest, lane)
        count = count * 2
    for d in range(local):
        rows[d] = state[0][d][: chunks + 1]

    @pl.when(m < slots - 1)
    def _():
        pl.semaphore_wait(barrier, 2 * bands - 1)

    @pl.when(m == slots - 1)
    def _():
        pl.semaphore_wait(barrier, bands - 1)

    def here_copy(j):
        to = lax.rem(k + j, bands)
        return pltpu.make_async_remote_copy(
            src_ref=rows.at[pl.ds(to * each, each)], dst_ref=here.at[k],
            send_sem=sems.at[0], recv_sem=sems.at[1],
            device_id=(to, m), device_id_type=MESH,
        )

    def next_copy(j):
        to = lax.rem(k + j, bands)
        return pltpu.make_async_remote_copy(
            src_ref=rows.at[pl.ds(to * each, each)], dst_ref=before.at[k],
            send_sem=sems.at[2], recv_sem=sems.at[3],
            device_id=(to, m + 1), device_id_type=MESH,
        )

    def all_of(blocks, sem):
        return pltpu.make_async_remote_copy(
            src_ref=blocks, dst_ref=blocks, send_sem=sem, recv_sem=sem,
            device_id=(k, m), device_id_type=MESH,
        )

    others = pl.ds(0, bands - 1)
    order = sorted(range(bands), key=lambda j: -min(j, bands - j))

    @pl.when(m < slots - 1)
    def _():
        for j in order:
            next_copy(j).start()

    for j in order:
        if j > 0:
            here_copy(j).start()
    here[k] = rows[pl.ds(k * each, each)]

    all_of(here.at[others], sems.at[1]).wait_recv()

    @pl.when(m > 0)
    def _():
        all_of(before, sems.at[3]).wait_recv()

    state = []
    for s in range(bands):
        trials = []
        for i in range(each):
            own, old = here[s, i], before[s, i]
            joint = own[:1] + old[chunks:]
            trials.append(jnp.concatenate([old[:chunks], joint, own[1:chunks]], axis=0))
        state.append(trials)
    width = each
    while count <= all_trials:
        width = width * 2
        state = merged(state, count, k * width, 0, all_trials, share, rest, lane)
        count = count * 2

    def part_copy(j, i):
        span_rows = pl.ds(cuts[i], cuts[i + 1] - cuts[i])
        return pltpu.make_async_remote_copy(
            src_ref=part.at[span_rows], dst_ref=parts.at[k, span_rows],
            send_sem=part_sems.at[0, i], recv_sem=part_sems.at[1, i],
            device_id=(lax.rem(k + j, bands), m), device_id_type=MESH,
        )

    def part_of_others(i):
        return parts.at[others, pl.ds(cuts[i], cuts[i + 1] - cuts[i])]

    window = state[0]
    sent = 0
    used = WIDTHS * chunks
    part[used:] = jnp.zeros((part.shape[0] - used, LANES), jnp.float32)
    for level in range(WIDTHS):
        w = 2**level
        peak = functools.reduce(jnp.maximum, window)[chunks:]
        part[level * chunks : (level + 1) * chunks] = peak * (
            1.0 / math.sqrt(all_trials * SUMMED * w)
        )
        if (level + 1) * chunks == cuts[sent + 1] or level + 1 == WIDTHS:
            for j in order:
                if j > 0:
                    part_copy(j, sent).start()
            sent = sent + 1
        if level + 1 < WIDTHS:
            later = []
            for row in window:
                above = pltpu.roll(row, 1, 0)
                if w < LANES:
                    above = moved(row, above, w, lane)
                later.append(row + above)
            window = later
    all_of(here.at[others], sems.at[0]).wait_send()

    @pl.when(m < slots - 1)
    def _():
        all_of(before, sems.at[2]).wait_send()

    parts[k] = part[...]
    for i in range(len(cuts) - 1):
        all_of(part_of_others(i), part_sems.at[1, i]).wait_recv()
        best = functools.reduce(
            jnp.maximum, [parts[s, cuts[i] : cuts[i + 1]] for s in range(bands)]
        )
        for flat in range(cuts[i], min(cuts[i + 1], used)):
            at = flat % chunks * LANES
            best_ref[flat // chunks : flat // chunks + 1, at : at + LANES] = best[
                flat - cuts[i] : flat - cuts[i] + 1
            ]
    for i in range(len(cuts) - 1):
        all_of(part_of_others(i), part_sems.at[0, i]).wait_send()


def one_block_back(mesh, channels, span, all_trials):
    bands = mesh.shape["freq"]
    local = channels // bands // SUMMED
    if span * 2 != SUBLANES * LANES or all_trials > LANES or local % bands != 0:
        return False
    reach = sum(2**level - 1 for level in range(1, all_trials.bit_length()))
    return reach + 2 ** (WIDTHS - 1) - 1 <= span


def shards_one_back(bands, slots, spectrogram, low_share, jitter):
    depth, span = spectrogram.shape
    all_trials = low_share.shape[0] + 1
    local = depth // SUMMED
    chunks = span // LANES
    each = local // bands
    cuts = (0, 16, -(-WIDTHS * chunks // SUBLANES) * SUBLANES)
    vmem = lambda *shape: pltpu.VMEM(shape, jnp.float32)
    return pl.pallas_call(
        functools.partial(search, bands, slots, all_trials, cuts),
        out_shape=jax.ShapeDtypeStruct((WIDTHS, span), jnp.float32),
        in_specs=[pl.BlockSpec(memory_space=pltpu.HBM)] * 3,
        out_specs=pl.BlockSpec(memory_space=pltpu.VMEM),
        scratch_shapes=[
            pltpu.VMEM((depth, span), spectrogram.dtype),
            pltpu.SMEM(low_share.shape, jnp.int32),
            pltpu.SMEM(jitter.shape, jnp.int32),
            vmem(local, SUBLANES, LANES),
            vmem(local, chunks + 1, LANES),
            vmem(bands, each, chunks + 1, LANES),
            vmem(bands, each, chunks + 1, LANES),
            vmem(cuts[-1], LANES),
            vmem(bands, cuts[-1], LANES),
            pltpu.SemaphoreType.DMA((4,)),
            pltpu.SemaphoreType.DMA((4,)),
            pltpu.SemaphoreType.DMA((2, len(cuts) - 1)),
        ],
        compiler_params=pltpu.CompilerParams(collective_id=0, has_side_effects=True),
    )(spectrogram, low_share, jitter)


def solution(mesh):
    placed = (P("freq", "tm"), P(), P())
    bands, slots = mesh.shape["freq"], mesh.shape["tm"]

    def run(spectrogram, low_share, jitter):
        channels, time = spectrogram.shape
        body = shards_any_reach
        if one_block_back(mesh, channels, time // slots, low_share.shape[0] + 1):
            body = functools.partial(shards_one_back, bands, slots)
        return jax.shard_map(
            body, mesh=mesh, in_specs=placed, out_specs=P(None, "tm"), check_vma=False
        )(spectrogram, low_share, jitter)

    return run
```

```python
import functools
import math

import jax
import jax.numpy as jnp
from jax import lax
from jax.experimental import pallas as pl
from jax.experimental.pallas import tpu as pltpu
from jax.sharding import PartitionSpec as P

SUMMED = 32
WIDTHS = 9
LANES = 128
SUBLANES = 8
MESH = pl.DeviceIdType.MESH


def passed_along(block, axis, distance):
    devices = range(lax.axis_size(axis))
    route = [(i - distance, i) for i in devices if i - distance in devices]
    return lax.ppermute(block, axis, route)


def swapped(block, axis, apart):
    count = lax.axis_size(axis)
    route = []
    for low in range(count):
        high = low | 1 << apart
        if high != low and high < count:
            route += [(low, high), (high, low)]
    return lax.ppermute(block, axis, route)


def widen(trial_rows, fetch_width):
    if fetch_width == 0:
        return trial_rows
    span_time = trial_rows.shape[-1]
    hop_count = min(-(-fetch_width // span_time), lax.axis_size("tm") - 1)
    pieces = [trial_rows]
    fetched = 0
    for hop_index in range(1, hop_count + 1):
        taken_cols = min(span_time, fetch_width - fetched)
        arrived = passed_along(trial_rows[..., span_time - taken_cols :], "tm", hop_index)
        pieces.insert(0, arrived)
        fetched = fetched + taken_cols
    if fetched < fetch_width:
        pieces.insert(
            0, jnp.zeros(trial_rows.shape[:-1] + (fetch_width - fetched,), trial_rows.dtype)
        )
    return jnp.concatenate(pieces, axis=-1)


def align_pair(low_set, high_set, margin, need_now, fetch_width):
    if fetch_width == 0:
        return (low_set[..., need_now:], high_set, margin - need_now)
    high_set = widen(high_set, fetch_width)
    low_set = widen(low_set, fetch_width - need_now)
    return (low_set, high_set, fetch_width - need_now)


def delay_of(trial_ids, subband_ids, trial_count, low_share, jitter):
    all_trials = low_share.shape[0] + 1
    rate_rows = jnp.take(low_share, all_trials // trial_count - 1 + subband_ids)
    return (trial_ids * rate_rows + jnp.take(jitter, trial_count - 2 + trial_ids)) // 64


def merge_rows(low_rows, high_rows, shifts, need_now):
    offsets = need_now - shifts
    bit_count = max(need_now.bit_length(), 1)
    moved = high_rows
    for bit_index in range(bit_count):
        step_size = 2**bit_index
        cols = moved.shape[-1]
        selected = (offsets >> bit_index & 1)[:, None] == 1
        moved = jnp.where(selected, moved[:, step_size:], moved[:, : cols - step_size])
    return low_rows + moved


def shards_any_reach(spectrogram, low_share, jitter):
    trial_dev = spectrogram.shape[0] // SUMMED
    span_time = spectrogram.shape[1]
    all_trials = low_share.shape[0] + 1
    freq_bits = lax.axis_size("freq").bit_length() - 1
    device = lax.axis_index("freq")
    local_counts = []
    trial_count = 2
    while trial_count <= trial_dev:
        local_counts.append(trial_count)
        trial_count = trial_count * 2
    cross_counts = [trial_dev * 2 ** (bit_index + 1) for bit_index in range(freq_bits)]
    need_list = [count_now - 1 for count_now in local_counts + cross_counts] + [
        2 ** (WIDTHS - 1) - 1
    ]
    fetch_plan = []
    margin = 0
    for position in range(len(need_list)):
        need_now = need_list[position]
        if margin >= need_now:
            fetch_plan.append(0)
            margin = margin - need_now
            continue
        fetch_width = need_now
        for later_need in need_list[position + 1 :]:
            if fetch_width + later_need > span_time:
                break
            fetch_width = fetch_width + later_need
        fetch_plan.append(fetch_width)
        margin = fetch_width - need_now
    states = jnp.sum(spectrogram.reshape(trial_dev, SUMMED, span_time), axis=1, dtype=jnp.float32)[
        :, None, :
    ]
    margin = 0
    section_index = 0
    for trial_count in local_counts:
        need_now = trial_count - 1
        groups = states.shape[0] // 2
        low_set, high_set, margin = align_pair(
            states[0::2], states[1::2], margin, need_now, fetch_plan[section_index]
        )
        low_rows = jnp.repeat(low_set, 2, axis=1).reshape(groups * trial_count, -1)
        high_rows = jnp.repeat(high_set, 2, axis=1).reshape(groups * trial_count, -1)
        trial_ids = jnp.tile(jnp.arange(trial_count, dtype=jnp.int32), groups)
        subband_ids = device * (trial_dev // trial_count) + jnp.repeat(
            jnp.arange(groups, dtype=jnp.int32), trial_count
        )
        shifts = delay_of(trial_ids, subband_ids, trial_count, low_share, jitter)
        states = merge_rows(low_rows, high_rows, shifts, need_now).reshape(groups, trial_count, -1)
        section_index = section_index + 1
    trial_rows = states[0]
    trial_ids = jnp.arange(trial_dev, dtype=jnp.int32)
    for bit_index in range(freq_bits):
        trial_count = cross_counts[bit_index]
        need_now = trial_count - 1
        partner = swapped(trial_rows, "freq", bit_index)
        upper_half = device >> bit_index & 1
        low_rows = jnp.where(upper_half == 1, partner, trial_rows)
        high_rows = jnp.where(upper_half == 1, trial_rows, partner)
        low_rows, high_rows, margin = align_pair(
            low_rows, high_rows, margin, need_now, fetch_plan[section_index]
        )
        trial_ids = 2 * trial_ids + upper_half
        shifts = delay_of(trial_ids, device >> bit_index + 1, trial_count, low_share, jitter)
        trial_rows = merge_rows(low_rows, high_rows, shifts, need_now)
        section_index = section_index + 1
    if fetch_plan[section_index] > 0:
        trial_rows = widen(trial_rows, fetch_plan[section_index])
    signal = trial_rows / math.sqrt(all_trials * SUMMED)
    peak_rows = []
    window_sum = signal
    width_now = 1
    for level_index in range(WIDTHS):
        length = window_sum.shape[1]
        peak_rows.append(
            jnp.max(window_sum[:, length - span_time :], axis=0) / math.sqrt(width_now)
        )
        if level_index + 1 < WIDTHS:
            window_sum = window_sum[:, width_now:] + window_sum[:, : length - width_now]
            width_now = width_now * 2
    local_best = jnp.stack(peak_rows)
    return lax.pmax(local_best, "freq")


def moved(row, above, delay, lane):
    return pltpu.roll(jnp.where(lane >= LANES - delay, above, row), delay, 1)


def merged(old, count, first_trial, first_subband, all_trials, share, rest, lane):
    new = []
    for s in range(len(old) // 2):
        rate = share[all_trials // count - 1 + first_subband + s]
        highs = [(row, pltpu.roll(row, 1, 0)) for row in old[2 * s + 1]]
        trials = []
        for j in range(2 * len(highs)):
            trial = first_trial + j
            delay = (trial * rate + rest[count - 2 + trial]) >> 6
            trials.append(old[2 * s][j // 2] + moved(*highs[j // 2], delay, lane))
        new.append(trials)
    return new


def search(
    bands, slots, all_trials, cuts,
    spec_hbm, share, rest, best_ref,
    spec, base_rows, rows, here, before, part, parts,
    in_sem, sems, part_sems,
):
    k, m = lax.axis_index("freq"), lax.axis_index("tm")
    span = spec.shape[1]
    chunks = span // LANES
    local = spec.shape[0] // SUMMED
    each = local // bands

    half = local // 2
    spec_loads = []
    for i in range(2):
        channels = pl.ds(i * half * SUMMED, half * SUMMED)
        spec_loads.append(
            pltpu.make_async_copy(spec_hbm.at[channels], spec.at[channels], in_sem.at[i])
        )
    for load in spec_loads:
        load.start()

    barrier = pltpu.get_barrier_semaphore()
    for j in range(1, bands):
        pl.semaphore_signal(
            barrier, inc=1, device_id=(lax.rem(k + j, bands), m), device_id_type=MESH
        )

    @pl.when(m > 0)
    def _():
        for j in range(bands):
            pl.semaphore_signal(
                barrier, inc=1, device_id=(lax.rem(k + j, bands), m - 1), device_id_type=MESH
            )

    lane = lax.broadcasted_iota(jnp.int32, (SUBLANES, LANES), 1)
    base_rows[...] = jnp.zeros_like(base_rows)

    @pl.when(m == 0)
    def _():
        before[...] = jnp.zeros_like(before)

    row_of = lax.broadcasted_iota(jnp.int32, (half, half * SUMMED), 0)
    channel = lax.broadcasted_iota(jnp.int32, (half, half * SUMMED), 1)
    ones = jnp.where(channel // SUMMED == row_of, 1.0, 0.0).astype(jnp.bfloat16)
    for i in range(2):
        spec_loads[i].wait()
        base = jnp.dot(
            ones,
            spec[i * half * SUMMED : (i + 1) * half * SUMMED],
            preferred_element_type=jnp.float32,
        )
        for q in range(chunks):
            base_rows[i * half : (i + 1) * half, q, :] = base[:, q * LANES : (q + 1) * LANES]
    state = [[base_rows[s]] for s in range(local)]
    count = 2
    while count <= local:
        state = merged(state, count, 0, k * (local // count), all_trials, share, rest, lane)
        count = count * 2
    for d in range(local):
        rows[d] = state[0][d][: chunks + 1]

    @pl.when(m < slots - 1)
    def _():
        pl.semaphore_wait(barrier, 2 * bands - 1)

    @pl.when(m == slots - 1)
    def _():
        pl.semaphore_wait(barrier, bands - 1)

    def here_copy(j):
        to = lax.rem(k + j, bands)
        return pltpu.make_async_remote_copy(
            src_ref=rows.at[pl.ds(to * each, each)], dst_ref=here.at[k],
            send_sem=sems.at[0], recv_sem=sems.at[1],
            device_id=(to, m), device_id_type=MESH,
        )

    def next_copy(j):
        to = lax.rem(k + j, bands)
        return pltpu.make_async_remote_copy(
            src_ref=rows.at[pl.ds(to * each, each)], dst_ref=before.at[k],
            send_sem=sems.at[2], recv_sem=sems.at[3],
            device_id=(to, m + 1), device_id_type=MESH,
        )

    def all_of(blocks, sem):
        return pltpu.make_async_remote_copy(
            src_ref=blocks, dst_ref=blocks, send_sem=sem, recv_sem=sem,
            device_id=(k, m), device_id_type=MESH,
        )

    others = pl.ds(0, bands - 1)
    order = sorted(range(bands), key=lambda j: -min(j, bands - j))

    @pl.when(m < slots - 1)
    def _():
        for j in order:
            next_copy(j).start()

    for j in order:
        if j > 0:
            here_copy(j).start()
    here[k] = rows[pl.ds(k * each, each)]

    all_of(here.at[others], sems.at[1]).wait_recv()

    @pl.when(m > 0)
    def _():
        all_of(before, sems.at[3]).wait_recv()

    state = []
    for s in range(bands):
        trials = []
        for i in range(each):
            own, old = here[s, i], before[s, i]
            joint = own[:1] + old[chunks:]
            trials.append(jnp.concatenate([old[:chunks], joint, own[1:chunks]], axis=0))
        state.append(trials)
    width = each
    while count <= all_trials:
        width = width * 2
        state = merged(state, count, k * width, 0, all_trials, share, rest, lane)
        count = count * 2

    def part_copy(j, i):
        span_rows = pl.ds(cuts[i], cuts[i + 1] - cuts[i])
        return pltpu.make_async_remote_copy(
            src_ref=part.at[span_rows], dst_ref=parts.at[k, span_rows],
            send_sem=part_sems.at[0, i], recv_sem=part_sems.at[1, i],
            device_id=(lax.rem(k + j, bands), m), device_id_type=MESH,
        )

    def part_of_others(i):
        return parts.at[others, pl.ds(cuts[i], cuts[i + 1] - cuts[i])]

    window = state[0]
    sent = 0
    used = WIDTHS * chunks
    part[used:] = jnp.zeros((part.shape[0] - used, LANES), jnp.float32)
    for level in range(WIDTHS):
        w = 2**level
        peak = functools.reduce(jnp.maximum, window)[chunks:]
        part[level * chunks : (level + 1) * chunks] = peak * (
            1.0 / math.sqrt(all_trials * SUMMED * w)
        )
        if (level + 1) * chunks == cuts[sent + 1] or level + 1 == WIDTHS:
            for j in order:
                if j > 0:
                    part_copy(j, sent).start()
            sent = sent + 1
        if level + 1 < WIDTHS:
            later = []
            for row in window:
                above = pltpu.roll(row, 1, 0)
                if w < LANES:
                    above = moved(row, above, w, lane)
                later.append(row + above)
            window = later
    all_of(here.at[others], sems.at[0]).wait_send()

    @pl.when(m < slots - 1)
    def _():
        all_of(before, sems.at[2]).wait_send()

    parts[k] = part[...]
    for i in range(len(cuts) - 1):
        all_of(part_of_others(i), part_sems.at[1, i]).wait_recv()
        best = functools.reduce(
            jnp.maximum, [parts[s, cuts[i] : cuts[i + 1]] for s in range(bands)]
        )
        for flat in range(cuts[i], min(cuts[i + 1], used)):
            at = flat % chunks * LANES
            best_ref[flat // chunks : flat // chunks + 1, at : at + LANES] = best[
                flat - cuts[i] : flat - cuts[i] + 1
            ]
    for i in range(len(cuts) - 1):
        all_of(part_of_others(i), part_sems.at[0, i]).wait_send()


def one_block_back(mesh, channels, span, all_trials):
    bands = mesh.shape["freq"]
    local = channels // bands // SUMMED
    if span * 2 != SUBLANES * LANES or all_trials > LANES or local % bands != 0:
        return False
    reach = sum(2**level - 1 for level in range(1, all_trials.bit_length()))
    return reach + 2 ** (WIDTHS - 1) - 1 <= span


def shards_one_back(bands, slots, spectrogram, low_share, jitter):
    depth, span = spectrogram.shape
    all_trials = low_share.shape[0] + 1
    local = depth // SUMMED
    chunks = span // LANES
    each = local // bands
    cuts = (0, 16, -(-WIDTHS * chunks // SUBLANES) * SUBLANES)
    vmem = lambda *shape: pltpu.VMEM(shape, jnp.float32)
    return pl.pallas_call(
        functools.partial(search, bands, slots, all_trials, cuts),
        out_shape=jax.ShapeDtypeStruct((WIDTHS, span), jnp.float32),
        in_specs=[pl.BlockSpec(memory_space=pl.ANY)]
        + [pl.BlockSpec(memory_space=pltpu.SMEM)] * 2,
        out_specs=pl.BlockSpec(memory_space=pltpu.VMEM),
        scratch_shapes=[
            pltpu.VMEM((depth, span), spectrogram.dtype),
            vmem(local, SUBLANES, LANES),
            vmem(local, chunks + 1, LANES),
            vmem(bands, each, chunks + 1, LANES),
            vmem(bands, each, chunks + 1, LANES),
            vmem(cuts[-1], LANES),
            vmem(bands, cuts[-1], LANES),
            pltpu.SemaphoreType.DMA((2,)),
            pltpu.SemaphoreType.DMA((4,)),
            pltpu.SemaphoreType.DMA((2, len(cuts) - 1)),
        ],
        compiler_params=pltpu.CompilerParams(
            collective_id=0, has_side_effects=True, vmem_limit_bytes=63225856
        ),
    )(spectrogram, low_share, jitter)


def solution(mesh):
    placed = (P("freq", "tm"), P(), P())
    bands, slots = mesh.shape["freq"], mesh.shape["tm"]

    def run(spectrogram, low_share, jitter):
        channels, time = spectrogram.shape
        body = shards_any_reach
        if one_block_back(mesh, channels, time // slots, low_share.shape[0] + 1):
            body = functools.partial(shards_one_back, bands, slots)
        return jax.shard_map(
            body, mesh=mesh, in_specs=placed, out_specs=P(None, "tm"), check_vma=False
        )(spectrogram, low_share, jitter)

    return run
```

```python
import functools
import math

import jax
import jax.numpy as jnp
from jax import lax
from jax.experimental import pallas as pl
from jax.experimental.pallas import tpu as pltpu
from jax.sharding import PartitionSpec as P

SUMMED = 32
WIDTHS = 9
LANES = 128
SUBLANES = 8
MESH = pl.DeviceIdType.MESH


def passed_along(block, axis, distance):
    devices = range(lax.axis_size(axis))
    route = [(i - distance, i) for i in devices if i - distance in devices]
    return lax.ppermute(block, axis, route)


def swapped(block, axis, apart):
    count = lax.axis_size(axis)
    route = []
    for low in range(count):
        high = low | 1 << apart
        if high != low and high < count:
            route += [(low, high), (high, low)]
    return lax.ppermute(block, axis, route)


def widen(trial_rows, fetch_width):
    if fetch_width == 0:
        return trial_rows
    span_time = trial_rows.shape[-1]
    hop_count = min(-(-fetch_width // span_time), lax.axis_size("tm") - 1)
    pieces = [trial_rows]
    fetched = 0
    for hop_index in range(1, hop_count + 1):
        taken_cols = min(span_time, fetch_width - fetched)
        arrived = passed_along(trial_rows[..., span_time - taken_cols :], "tm", hop_index)
        pieces.insert(0, arrived)
        fetched = fetched + taken_cols
    if fetched < fetch_width:
        pieces.insert(
            0, jnp.zeros(trial_rows.shape[:-1] + (fetch_width - fetched,), trial_rows.dtype)
        )
    return jnp.concatenate(pieces, axis=-1)


def align_pair(low_set, high_set, margin, need_now, fetch_width):
    if fetch_width == 0:
        return (low_set[..., need_now:], high_set, margin - need_now)
    high_set = widen(high_set, fetch_width)
    low_set = widen(low_set, fetch_width - need_now)
    return (low_set, high_set, fetch_width - need_now)


def delay_of(trial_ids, subband_ids, trial_count, low_share, jitter):
    all_trials = low_share.shape[0] + 1
    rate_rows = jnp.take(low_share, all_trials // trial_count - 1 + subband_ids)
    return (trial_ids * rate_rows + jnp.take(jitter, trial_count - 2 + trial_ids)) // 64


def merge_rows(low_rows, high_rows, shifts, need_now):
    offsets = need_now - shifts
    bit_count = max(need_now.bit_length(), 1)
    moved = high_rows
    for bit_index in range(bit_count):
        step_size = 2**bit_index
        cols = moved.shape[-1]
        selected = (offsets >> bit_index & 1)[:, None] == 1
        moved = jnp.where(selected, moved[:, step_size:], moved[:, : cols - step_size])
    return low_rows + moved


def shards_any_reach(spectrogram, low_share, jitter):
    trial_dev = spectrogram.shape[0] // SUMMED
    span_time = spectrogram.shape[1]
    all_trials = low_share.shape[0] + 1
    freq_bits = lax.axis_size("freq").bit_length() - 1
    device = lax.axis_index("freq")
    local_counts = []
    trial_count = 2
    while trial_count <= trial_dev:
        local_counts.append(trial_count)
        trial_count = trial_count * 2
    cross_counts = [trial_dev * 2 ** (bit_index + 1) for bit_index in range(freq_bits)]
    need_list = [count_now - 1 for count_now in local_counts + cross_counts] + [
        2 ** (WIDTHS - 1) - 1
    ]
    fetch_plan = []
    margin = 0
    for position in range(len(need_list)):
        need_now = need_list[position]
        if margin >= need_now:
            fetch_plan.append(0)
            margin = margin - need_now
            continue
        fetch_width = need_now
        for later_need in need_list[position + 1 :]:
            if fetch_width + later_need > span_time:
                break
            fetch_width = fetch_width + later_need
        fetch_plan.append(fetch_width)
        margin = fetch_width - need_now
    states = jnp.sum(spectrogram.reshape(trial_dev, SUMMED, span_time), axis=1, dtype=jnp.float32)[
        :, None, :
    ]
    margin = 0
    section_index = 0
    for trial_count in local_counts:
        need_now = trial_count - 1
        groups = states.shape[0] // 2
        low_set, high_set, margin = align_pair(
            states[0::2], states[1::2], margin, need_now, fetch_plan[section_index]
        )
        low_rows = jnp.repeat(low_set, 2, axis=1).reshape(groups * trial_count, -1)
        high_rows = jnp.repeat(high_set, 2, axis=1).reshape(groups * trial_count, -1)
        trial_ids = jnp.tile(jnp.arange(trial_count, dtype=jnp.int32), groups)
        subband_ids = device * (trial_dev // trial_count) + jnp.repeat(
            jnp.arange(groups, dtype=jnp.int32), trial_count
        )
        shifts = delay_of(trial_ids, subband_ids, trial_count, low_share, jitter)
        states = merge_rows(low_rows, high_rows, shifts, need_now).reshape(groups, trial_count, -1)
        section_index = section_index + 1
    trial_rows = states[0]
    trial_ids = jnp.arange(trial_dev, dtype=jnp.int32)
    for bit_index in range(freq_bits):
        trial_count = cross_counts[bit_index]
        need_now = trial_count - 1
        partner = swapped(trial_rows, "freq", bit_index)
        upper_half = device >> bit_index & 1
        low_rows = jnp.where(upper_half == 1, partner, trial_rows)
        high_rows = jnp.where(upper_half == 1, trial_rows, partner)
        low_rows, high_rows, margin = align_pair(
            low_rows, high_rows, margin, need_now, fetch_plan[section_index]
        )
        trial_ids = 2 * trial_ids + upper_half
        shifts = delay_of(trial_ids, device >> bit_index + 1, trial_count, low_share, jitter)
        trial_rows = merge_rows(low_rows, high_rows, shifts, need_now)
        section_index = section_index + 1
    if fetch_plan[section_index] > 0:
        trial_rows = widen(trial_rows, fetch_plan[section_index])
    signal = trial_rows / math.sqrt(all_trials * SUMMED)
    peak_rows = []
    window_sum = signal
    width_now = 1
    for level_index in range(WIDTHS):
        length = window_sum.shape[1]
        peak_rows.append(
            jnp.max(window_sum[:, length - span_time :], axis=0) / math.sqrt(width_now)
        )
        if level_index + 1 < WIDTHS:
            window_sum = window_sum[:, width_now:] + window_sum[:, : length - width_now]
            width_now = width_now * 2
    local_best = jnp.stack(peak_rows)
    return lax.pmax(local_best, "freq")


def moved(row, above, delay, lane):
    return pltpu.roll(jnp.where(lane >= LANES - delay, above, row), delay, 1)


def delays_of(subbands, trials, count, first_trial, first_subband, all_trials, share, rest):
    jitters = [rest[count - 2 + first_trial + j] for j in range(trials)]
    delays = []
    for s in range(subbands):
        rate = share[all_trials // count - 1 + first_subband + s]
        delays.append([((first_trial + j) * rate + jitters[j]) >> 6 for j in range(trials)])
    return delays


def merged(old, delays, lane):
    new = []
    for s in range(len(old) // 2):
        highs = [(row, pltpu.roll(row, 1, 0)) for row in old[2 * s + 1]]
        new.append(
            [
                old[2 * s][j // 2] + moved(*highs[j // 2], delays[s][j], lane)
                for j in range(2 * len(highs))
            ]
        )
    return new


def search(
    bands, slots, all_trials, cuts,
    spec_hbm, share_hbm, rest_hbm, best_ref,
    spec, share, rest, later_delays, base_rows, rows, here, before, part, parts,
    in_sem, sems, part_sems,
):
    k, m = lax.axis_index("freq"), lax.axis_index("tm")
    span = spec.shape[1]
    chunks = span // LANES
    local = spec.shape[0] // SUMMED
    each = local // bands

    half = local // 2
    spec_loads = []
    for i in range(2):
        channels = pl.ds(i * half * SUMMED, half * SUMMED)
        spec_loads.append(
            pltpu.make_async_copy(spec_hbm.at[channels], spec.at[channels], in_sem.at[i])
        )
    table_loads = [
        pltpu.make_async_copy(share_hbm, share, in_sem.at[2]),
        pltpu.make_async_copy(rest_hbm, rest, in_sem.at[3]),
    ]
    for load in spec_loads + table_loads:
        load.start()

    barrier = pltpu.get_barrier_semaphore()
    for j in range(1, bands):
        pl.semaphore_signal(
            barrier, inc=1, device_id=(lax.rem(k + j, bands), m), device_id_type=MESH
        )

    @pl.when(m > 0)
    def _():
        for j in range(bands):
            pl.semaphore_signal(
                barrier, inc=1, device_id=(lax.rem(k + j, bands), m - 1), device_id_type=MESH
            )

    lane = lax.broadcasted_iota(jnp.int32, (SUBLANES, LANES), 1)
    base_rows[...] = jnp.zeros_like(base_rows)

    @pl.when(m == 0)
    def _():
        before[...] = jnp.zeros_like(before)

    row_of = lax.broadcasted_iota(jnp.int32, (half, half * SUMMED), 0)
    channel = lax.broadcasted_iota(jnp.int32, (half, half * SUMMED), 1)
    ones = jnp.where(channel // SUMMED == row_of, 1.0, 0.0).astype(jnp.bfloat16)
    for i in range(2):
        spec_loads[i].wait()
        base = jnp.dot(
            ones,
            spec[i * half * SUMMED : (i + 1) * half * SUMMED],
            preferred_element_type=jnp.float32,
        )
        for q in range(chunks):
            base_rows[i * half : (i + 1) * half, q, :] = base[:, q * LANES : (q + 1) * LANES]
    for load in table_loads:
        load.wait()
    state = [[base_rows[s]] for s in range(local)]
    count = 2
    while count <= local:
        groups = local // count
        delays = delays_of(groups, count, count, 0, k * groups, all_trials, share, rest)
        state = merged(state, delays, lane)
        count = count * 2
    for d in range(local):
        rows[d] = state[0][d][: chunks + 1]

    @pl.when(m < slots - 1)
    def _():
        pl.semaphore_wait(barrier, 2 * bands - 1)

    @pl.when(m == slots - 1)
    def _():
        pl.semaphore_wait(barrier, bands - 1)

    kept = pl.ds(0, chunks)

    def here_copy(j):
        to = lax.rem(k + j, bands)
        return pltpu.make_async_remote_copy(
            src_ref=rows.at[pl.ds(to * each, each), kept], dst_ref=here.at[k, :, kept],
            send_sem=sems.at[0], recv_sem=sems.at[1],
            device_id=(to, m), device_id_type=MESH,
        )

    def next_copy(j):
        to = lax.rem(k + j, bands)
        return pltpu.make_async_remote_copy(
            src_ref=rows.at[pl.ds(to * each, each)], dst_ref=before.at[k],
            send_sem=sems.at[2], recv_sem=sems.at[3],
            device_id=(to, m + 1), device_id_type=MESH,
        )

    def all_of(blocks, sem):
        return pltpu.make_async_remote_copy(
            src_ref=blocks, dst_ref=blocks, send_sem=sem, recv_sem=sem,
            device_id=(k, m), device_id_type=MESH,
        )

    others = pl.ds(0, bands - 1)
    order = sorted(range(bands), key=lambda j: -min(j, bands - j))

    @pl.when(m < slots - 1)
    def _():
        for j in order:
            next_copy(j).start()

    for j in order:
        if j > 0:
            here_copy(j).start()
    here[k, :, :chunks] = rows[pl.ds(k * each, each), :chunks]

    levels = []
    width, groups, flat = each, bands, 0
    while count <= all_trials:
        width, groups = width * 2, groups // 2
        level = delays_of(groups, width, count, k * width, 0, all_trials, share, rest)
        for s in range(groups):
            for j in range(width):
                later_delays[flat + s * width + j] = level[s][j]
        levels.append((groups, width, flat))
        flat = flat + groups * width
        count = count * 2

    all_of(here.at[others, :, kept], sems.at[1]).wait_recv()

    @pl.when(m > 0)
    def _():
        all_of(before, sems.at[3]).wait_recv()

    state = []
    for s in range(bands):
        trials = []
        for i in range(each):
            own, old = here[s, i, :chunks], before[s, i]
            joint = own[:1] + old[chunks:]
            trials.append(jnp.concatenate([old[:chunks], joint, own[1:]], axis=0))
        state.append(trials)
    for groups, width, flat in levels:
        delays = [[later_delays[flat + s * width + j] for j in range(width)] for s in range(groups)]
        state = merged(state, delays, lane)

    def part_copy(j, i):
        span_rows = pl.ds(cuts[i], cuts[i + 1] - cuts[i])
        return pltpu.make_async_remote_copy(
            src_ref=part.at[span_rows], dst_ref=parts.at[k, span_rows],
            send_sem=part_sems.at[0, i], recv_sem=part_sems.at[1, i],
            device_id=(lax.rem(k + j, bands), m), device_id_type=MESH,
        )

    def part_of_others(i):
        return parts.at[others, pl.ds(cuts[i], cuts[i + 1] - cuts[i])]

    window = state[0]
    sent = 0
    used = WIDTHS * chunks
    for level in range(WIDTHS):
        w = 2**level
        peak = functools.reduce(jnp.maximum, window)[chunks:]
        part[level * chunks : (level + 1) * chunks] = peak * (
            1.0 / math.sqrt(all_trials * SUMMED * w)
        )
        if (level + 1) * chunks == cuts[sent + 1] or level + 1 == WIDTHS:
            for j in order:
                if j > 0:
                    part_copy(j, sent).start()
            sent = sent + 1
        if level + 1 < WIDTHS:
            later = []
            for row in window:
                above = pltpu.roll(row, 1, 0)
                if w < LANES:
                    above = moved(row, above, w, lane)
                later.append(row + above)
            window = later
    all_of(here.at[others, :, kept], sems.at[0]).wait_send()

    @pl.when(m < slots - 1)
    def _():
        all_of(before, sems.at[2]).wait_send()

    parts[k] = part[...]
    for i in range(len(cuts) - 1):
        all_of(part_of_others(i), part_sems.at[1, i]).wait_recv()
        best = functools.reduce(
            jnp.maximum, [parts[s, cuts[i] : cuts[i + 1]] for s in range(bands)]
        )
        for flat in range(cuts[i], min(cuts[i + 1], used)):
            at = flat % chunks * LANES
            best_ref[flat // chunks : flat // chunks + 1, at : at + LANES] = best[
                flat - cuts[i] : flat - cuts[i] + 1
            ]
    for i in range(len(cuts) - 1):
        all_of(part_of_others(i), part_sems.at[0, i]).wait_send()


def one_block_back(mesh, channels, span, all_trials):
    bands = mesh.shape["freq"]
    local = channels // bands // SUMMED
    if span * 2 != SUBLANES * LANES or all_trials > LANES or local % bands != 0:
        return False
    reach = sum(2**level - 1 for level in range(1, all_trials.bit_length()))
    return reach + 2 ** (WIDTHS - 1) - 1 <= span


def shards_one_back(bands, slots, spectrogram, low_share, jitter):
    depth, span = spectrogram.shape
    all_trials = low_share.shape[0] + 1
    local = depth // SUMMED
    chunks = span // LANES
    each = local // bands
    cuts = (0, 16, WIDTHS * chunks)
    vmem = lambda *shape: pltpu.VMEM(shape, jnp.float32)
    return pl.pallas_call(
        functools.partial(search, bands, slots, all_trials, cuts),
        out_shape=jax.ShapeDtypeStruct((WIDTHS, span), jnp.float32),
        in_specs=[pl.BlockSpec(memory_space=pltpu.HBM)] * 3,
        out_specs=pl.BlockSpec(memory_space=pltpu.VMEM),
        scratch_shapes=[
            pltpu.VMEM((depth, span), spectrogram.dtype),
            pltpu.SMEM(low_share.shape, jnp.int32),
            pltpu.SMEM(jitter.shape, jnp.int32),
            pltpu.SMEM((all_trials,), jnp.int32),
            vmem(local, SUBLANES, LANES),
            vmem(local, chunks + 1, LANES),
            vmem(bands, each, chunks + 1, LANES),
            vmem(bands, each, chunks + 1, LANES),
            vmem(cuts[-1], LANES),
            vmem(bands, cuts[-1], LANES),
            pltpu.SemaphoreType.DMA((4,)),
            pltpu.SemaphoreType.DMA((4,)),
            pltpu.SemaphoreType.DMA((2, len(cuts) - 1)),
        ],
        compiler_params=pltpu.CompilerParams(collective_id=0, has_side_effects=True),
    )(spectrogram, low_share, jitter)


def solution(mesh):
    placed = (P("freq", "tm"), P(), P())
    bands, slots = mesh.shape["freq"], mesh.shape["tm"]

    def run(spectrogram, low_share, jitter):
        channels, time = spectrogram.shape
        body = shards_any_reach
        if one_block_back(mesh, channels, time // slots, low_share.shape[0] + 1):
            body = functools.partial(shards_one_back, bands, slots)
        return jax.shard_map(
            body, mesh=mesh, in_specs=placed, out_specs=P(None, "tm"), check_vma=False
        )(spectrogram, low_share, jitter)

    return run
```

```python
import functools
import math

import jax
import jax.numpy as jnp
from jax import lax
from jax.experimental import pallas as pl
from jax.experimental.pallas import tpu as pltpu
from jax.sharding import PartitionSpec as P

SUMMED = 32
WIDTHS = 9
LANES = 128
SUBLANES = 8
MESH = pl.DeviceIdType.MESH


def passed_along(block, axis, distance):
    devices = range(lax.axis_size(axis))
    route = [(i - distance, i) for i in devices if i - distance in devices]
    return lax.ppermute(block, axis, route)


def swapped(block, axis, apart):
    count = lax.axis_size(axis)
    route = []
    for low in range(count):
        high = low | 1 << apart
        if high != low and high < count:
            route += [(low, high), (high, low)]
    return lax.ppermute(block, axis, route)


def widen(trial_rows, fetch_width):
    if fetch_width == 0:
        return trial_rows
    span_time = trial_rows.shape[-1]
    hop_count = min(-(-fetch_width // span_time), lax.axis_size("tm") - 1)
    pieces = [trial_rows]
    fetched = 0
    for hop_index in range(1, hop_count + 1):
        taken_cols = min(span_time, fetch_width - fetched)
        arrived = passed_along(trial_rows[..., span_time - taken_cols :], "tm", hop_index)
        pieces.insert(0, arrived)
        fetched = fetched + taken_cols
    if fetched < fetch_width:
        pieces.insert(
            0, jnp.zeros(trial_rows.shape[:-1] + (fetch_width - fetched,), trial_rows.dtype)
        )
    return jnp.concatenate(pieces, axis=-1)


def align_pair(low_set, high_set, margin, need_now, fetch_width):
    if fetch_width == 0:
        return (low_set[..., need_now:], high_set, margin - need_now)
    high_set = widen(high_set, fetch_width)
    low_set = widen(low_set, fetch_width - need_now)
    return (low_set, high_set, fetch_width - need_now)


def delay_of(trial_ids, subband_ids, trial_count, low_share, jitter):
    all_trials = low_share.shape[0] + 1
    rate_rows = jnp.take(low_share, all_trials // trial_count - 1 + subband_ids)
    return (trial_ids * rate_rows + jnp.take(jitter, trial_count - 2 + trial_ids)) // 64


def merge_rows(low_rows, high_rows, shifts, need_now):
    offsets = need_now - shifts
    bit_count = max(need_now.bit_length(), 1)
    moved = high_rows
    for bit_index in range(bit_count):
        step_size = 2**bit_index
        cols = moved.shape[-1]
        selected = (offsets >> bit_index & 1)[:, None] == 1
        moved = jnp.where(selected, moved[:, step_size:], moved[:, : cols - step_size])
    return low_rows + moved


def shards_any_reach(spectrogram, low_share, jitter):
    trial_dev = spectrogram.shape[0] // SUMMED
    span_time = spectrogram.shape[1]
    all_trials = low_share.shape[0] + 1
    freq_bits = lax.axis_size("freq").bit_length() - 1
    device = lax.axis_index("freq")
    local_counts = []
    trial_count = 2
    while trial_count <= trial_dev:
        local_counts.append(trial_count)
        trial_count = trial_count * 2
    cross_counts = [trial_dev * 2 ** (bit_index + 1) for bit_index in range(freq_bits)]
    need_list = [count_now - 1 for count_now in local_counts + cross_counts] + [
        2 ** (WIDTHS - 1) - 1
    ]
    fetch_plan = []
    margin = 0
    for position in range(len(need_list)):
        need_now = need_list[position]
        if margin >= need_now:
            fetch_plan.append(0)
            margin = margin - need_now
            continue
        fetch_width = need_now
        for later_need in need_list[position + 1 :]:
            if fetch_width + later_need > span_time:
                break
            fetch_width = fetch_width + later_need
        fetch_plan.append(fetch_width)
        margin = fetch_width - need_now
    states = jnp.sum(spectrogram.reshape(trial_dev, SUMMED, span_time), axis=1, dtype=jnp.float32)[
        :, None, :
    ]
    margin = 0
    section_index = 0
    for trial_count in local_counts:
        need_now = trial_count - 1
        groups = states.shape[0] // 2
        low_set, high_set, margin = align_pair(
            states[0::2], states[1::2], margin, need_now, fetch_plan[section_index]
        )
        low_rows = jnp.repeat(low_set, 2, axis=1).reshape(groups * trial_count, -1)
        high_rows = jnp.repeat(high_set, 2, axis=1).reshape(groups * trial_count, -1)
        trial_ids = jnp.tile(jnp.arange(trial_count, dtype=jnp.int32), groups)
        subband_ids = device * (trial_dev // trial_count) + jnp.repeat(
            jnp.arange(groups, dtype=jnp.int32), trial_count
        )
        shifts = delay_of(trial_ids, subband_ids, trial_count, low_share, jitter)
        states = merge_rows(low_rows, high_rows, shifts, need_now).reshape(groups, trial_count, -1)
        section_index = section_index + 1
    trial_rows = states[0]
    trial_ids = jnp.arange(trial_dev, dtype=jnp.int32)
    for bit_index in range(freq_bits):
        trial_count = cross_counts[bit_index]
        need_now = trial_count - 1
        partner = swapped(trial_rows, "freq", bit_index)
        upper_half = device >> bit_index & 1
        low_rows = jnp.where(upper_half == 1, partner, trial_rows)
        high_rows = jnp.where(upper_half == 1, trial_rows, partner)
        low_rows, high_rows, margin = align_pair(
            low_rows, high_rows, margin, need_now, fetch_plan[section_index]
        )
        trial_ids = 2 * trial_ids + upper_half
        shifts = delay_of(trial_ids, device >> bit_index + 1, trial_count, low_share, jitter)
        trial_rows = merge_rows(low_rows, high_rows, shifts, need_now)
        section_index = section_index + 1
    if fetch_plan[section_index] > 0:
        trial_rows = widen(trial_rows, fetch_plan[section_index])
    signal = trial_rows / math.sqrt(all_trials * SUMMED)
    peak_rows = []
    window_sum = signal
    width_now = 1
    for level_index in range(WIDTHS):
        length = window_sum.shape[1]
        peak_rows.append(
            jnp.max(window_sum[:, length - span_time :], axis=0) / math.sqrt(width_now)
        )
        if level_index + 1 < WIDTHS:
            window_sum = window_sum[:, width_now:] + window_sum[:, : length - width_now]
            width_now = width_now * 2
    local_best = jnp.stack(peak_rows)
    return lax.pmax(local_best, "freq")


def moved(row, above, delay, lane):
    return pltpu.roll(jnp.where(lane >= LANES - delay, above, row), delay, 1)


def delays_of(subbands, trials, count, first_trial, first_subband, all_trials, share, rest):
    jitters = [rest[count - 2 + first_trial + j] for j in range(trials)]
    delays = []
    for s in range(subbands):
        rate = share[all_trials // count - 1 + first_subband + s]
        delays.append([((first_trial + j) * rate + jitters[j]) >> 6 for j in range(trials)])
    return delays


def merged(old, delays, lane):
    new = []
    for s in range(len(old) // 2):
        highs = [(row, pltpu.roll(row, 1, 0)) for row in old[2 * s + 1]]
        new.append(
            [
                old[2 * s][j // 2] + moved(*highs[j // 2], delays[s][j], lane)
                for j in range(2 * len(highs))
            ]
        )
    return new


def search(
    bands, slots, all_trials, cuts,
    spec_hbm, share_hbm, rest_hbm, best_ref,
    spec, share, rest, later_delays, base_rows, rows, here, before, part, parts,
    in_sem, sems, part_sems,
):
    k, m = lax.axis_index("freq"), lax.axis_index("tm")
    span = spec.shape[1]
    chunks = span // LANES
    local = spec.shape[0] // SUMMED
    each = local // bands

    half = local // 2
    spec_loads = []
    for i in range(2):
        channels = pl.ds(i * half * SUMMED, half * SUMMED)
        spec_loads.append(
            pltpu.make_async_copy(spec_hbm.at[channels], spec.at[channels], in_sem.at[i])
        )
    table_loads = [
        pltpu.make_async_copy(share_hbm, share, in_sem.at[2]),
        pltpu.make_async_copy(rest_hbm, rest, in_sem.at[3]),
    ]
    for load in spec_loads + table_loads:
        load.start()

    barrier = pltpu.get_barrier_semaphore()
    for j in range(1, bands):
        pl.semaphore_signal(
            barrier, inc=1, device_id=(lax.rem(k + j, bands), m), device_id_type=MESH
        )

    @pl.when(m > 0)
    def _():
        for j in range(bands):
            pl.semaphore_signal(
                barrier, inc=1, device_id=(lax.rem(k + j, bands), m - 1), device_id_type=MESH
            )

    lane = lax.broadcasted_iota(jnp.int32, (SUBLANES, LANES), 1)
    base_rows[...] = jnp.zeros_like(base_rows)

    @pl.when(m == 0)
    def _():
        before[...] = jnp.zeros_like(before)

    row_of = lax.broadcasted_iota(jnp.int32, (half, half * SUMMED), 0)
    channel = lax.broadcasted_iota(jnp.int32, (half, half * SUMMED), 1)
    ones = jnp.where(channel // SUMMED == row_of, 1.0, 0.0).astype(jnp.bfloat16)
    for i in range(2):
        spec_loads[i].wait()
        base = jnp.dot(
            ones,
            spec[i * half * SUMMED : (i + 1) * half * SUMMED],
            preferred_element_type=jnp.float32,
        )
        for q in range(chunks):
            base_rows[i * half : (i + 1) * half, q, :] = base[:, q * LANES : (q + 1) * LANES]
    for load in table_loads:
        load.wait()
    state = [[base_rows[s]] for s in range(local)]
    count = 2
    while count <= local:
        groups = local // count
        delays = delays_of(groups, count, count, 0, k * groups, all_trials, share, rest)
        state = merged(state, delays, lane)
        count = count * 2
    for d in range(local):
        rows[d] = state[0][d][: chunks + 1]

    @pl.when(m < slots - 1)
    def _():
        pl.semaphore_wait(barrier, 2 * bands - 1)

    @pl.when(m == slots - 1)
    def _():
        pl.semaphore_wait(barrier, bands - 1)

    kept = pl.ds(0, chunks)

    def here_copy(j):
        to = lax.rem(k + j, bands)
        return pltpu.make_async_remote_copy(
            src_ref=rows.at[pl.ds(to * each, each), kept], dst_ref=here.at[k, :, kept],
            send_sem=sems.at[0], recv_sem=sems.at[1],
            device_id=(to, m), device_id_type=MESH,
        )

    def next_copy(j):
        to = lax.rem(k + j, bands)
        return pltpu.make_async_remote_copy(
            src_ref=rows.at[pl.ds(to * each, each)], dst_ref=before.at[k],
            send_sem=sems.at[2], recv_sem=sems.at[3],
            device_id=(to, m + 1), device_id_type=MESH,
        )

    def all_of(blocks, sem):
        return pltpu.make_async_remote_copy(
            src_ref=blocks, dst_ref=blocks, send_sem=sem, recv_sem=sem,
            device_id=(k, m), device_id_type=MESH,
        )

    others = pl.ds(0, bands - 1)
    order = sorted(range(bands), key=lambda j: -min(j, bands - j))

    for j in order:
        if j > 0:
            here_copy(j).start()

    @pl.when(m < slots - 1)
    def _():
        for j in order:
            next_copy(j).start()

    here[k, :, :chunks] = rows[pl.ds(k * each, each), :chunks]

    levels = []
    width, groups, flat = each, bands, 0
    while count <= all_trials:
        width, groups = width * 2, groups // 2
        level = delays_of(groups, width, count, k * width, 0, all_trials, share, rest)
        for s in range(groups):
            for j in range(width):
                later_delays[flat + s * width + j] = level[s][j]
        levels.append((groups, width, flat))
        flat = flat + groups * width
        count = count * 2

    all_of(here.at[others, :, kept], sems.at[1]).wait_recv()

    @pl.when(m > 0)
    def _():
        all_of(before, sems.at[3]).wait_recv()

    state = []
    for s in range(bands):
        trials = []
        for i in range(each):
            own, old = here[s, i, :chunks], before[s, i]
            joint = own[:1] + old[chunks:]
            trials.append(jnp.concatenate([old[:chunks], joint, own[1:]], axis=0))
        state.append(trials)
    for groups, width, flat in levels:
        delays = [[later_delays[flat + s * width + j] for j in range(width)] for s in range(groups)]
        state = merged(state, delays, lane)

    def part_copy(j, i):
        span_rows = pl.ds(cuts[i], cuts[i + 1] - cuts[i])
        return pltpu.make_async_remote_copy(
            src_ref=part.at[span_rows], dst_ref=parts.at[k, span_rows],
            send_sem=part_sems.at[0, i], recv_sem=part_sems.at[1, i],
            device_id=(lax.rem(k + j, bands), m), device_id_type=MESH,
        )

    def part_of_others(i):
        return parts.at[others, pl.ds(cuts[i], cuts[i + 1] - cuts[i])]

    window = state[0]
    sent = 0
    used = WIDTHS * chunks
    for level in range(WIDTHS):
        w = 2**level
        peak = functools.reduce(jnp.maximum, window)[chunks:]
        part[level * chunks : (level + 1) * chunks] = peak * (
            1.0 / math.sqrt(all_trials * SUMMED * w)
        )
        if (level + 1) * chunks == cuts[sent + 1] or level + 1 == WIDTHS:
            for j in order:
                if j > 0:
                    part_copy(j, sent).start()
            sent = sent + 1
        if level + 1 < WIDTHS:
            later = []
            for row in window:
                above = pltpu.roll(row, 1, 0)
                if w < LANES:
                    above = moved(row, above, w, lane)
                later.append(row + above)
            window = later
    all_of(here.at[others, :, kept], sems.at[0]).wait_send()

    @pl.when(m < slots - 1)
    def _():
        all_of(before, sems.at[2]).wait_send()

    parts[k] = part[...]
    for i in range(len(cuts) - 1):
        all_of(part_of_others(i), part_sems.at[1, i]).wait_recv()
        best = functools.reduce(
            jnp.maximum, [parts[s, cuts[i] : cuts[i + 1]] for s in range(bands)]
        )
        for flat in range(cuts[i], min(cuts[i + 1], used)):
            at = flat % chunks * LANES
            best_ref[flat // chunks : flat // chunks + 1, at : at + LANES] = best[
                flat - cuts[i] : flat - cuts[i] + 1
            ]
    for i in range(len(cuts) - 1):
        all_of(part_of_others(i), part_sems.at[0, i]).wait_send()


def one_block_back(mesh, channels, span, all_trials):
    bands = mesh.shape["freq"]
    local = channels // bands // SUMMED
    if span * 2 != SUBLANES * LANES or all_trials > LANES or local % bands != 0:
        return False
    reach = sum(2**level - 1 for level in range(1, all_trials.bit_length()))
    return reach + 2 ** (WIDTHS - 1) - 1 <= span


def shards_one_back(bands, slots, spectrogram, low_share, jitter):
    depth, span = spectrogram.shape
    all_trials = low_share.shape[0] + 1
    local = depth // SUMMED
    chunks = span // LANES
    each = local // bands
    cuts = (0, 16, WIDTHS * chunks)
    vmem = lambda *shape: pltpu.VMEM(shape, jnp.float32)
    return pl.pallas_call(
        functools.partial(search, bands, slots, all_trials, cuts),
        out_shape=jax.ShapeDtypeStruct((WIDTHS, span), jnp.float32),
        in_specs=[pl.BlockSpec(memory_space=pltpu.HBM)] * 3,
        out_specs=pl.BlockSpec(memory_space=pltpu.VMEM),
        scratch_shapes=[
            pltpu.VMEM((depth, span), spectrogram.dtype),
            pltpu.SMEM(low_share.shape, jnp.int32),
            pltpu.SMEM(jitter.shape, jnp.int32),
            pltpu.SMEM((all_trials,), jnp.int32),
            vmem(local, SUBLANES, LANES),
            vmem(local, chunks + 1, LANES),
            vmem(bands, each, chunks + 1, LANES),
            vmem(bands, each, chunks + 1, LANES),
            vmem(cuts[-1], LANES),
            vmem(bands, cuts[-1], LANES),
            pltpu.SemaphoreType.DMA((4,)),
            pltpu.SemaphoreType.DMA((4,)),
            pltpu.SemaphoreType.DMA((2, len(cuts) - 1)),
        ],
        compiler_params=pltpu.CompilerParams(collective_id=0, has_side_effects=True),
    )(spectrogram, low_share, jitter)


def solution(mesh):
    placed = (P("freq", "tm"), P(), P())
    bands, slots = mesh.shape["freq"], mesh.shape["tm"]

    def run(spectrogram, low_share, jitter):
        channels, time = spectrogram.shape
        body = shards_any_reach
        if one_block_back(mesh, channels, time // slots, low_share.shape[0] + 1):
            body = functools.partial(shards_one_back, bands, slots)
        return jax.shard_map(
            body, mesh=mesh, in_specs=placed, out_specs=P(None, "tm"), check_vma=False
        )(spectrogram, low_share, jitter)

    return run
```

```python
import functools
import math

import jax
import jax.numpy as jnp
from jax import lax
from jax.experimental import pallas as pl
from jax.experimental.pallas import tpu as pltpu
from jax.sharding import PartitionSpec as P

SUMMED = 32
WIDTHS = 9
LANES = 128
SUBLANES = 8
MESH = pl.DeviceIdType.MESH


def passed_along(block, axis, distance):
    devices = range(lax.axis_size(axis))
    route = [(i - distance, i) for i in devices if i - distance in devices]
    return lax.ppermute(block, axis, route)


def swapped(block, axis, apart):
    count = lax.axis_size(axis)
    route = []
    for low in range(count):
        high = low | 1 << apart
        if high != low and high < count:
            route += [(low, high), (high, low)]
    return lax.ppermute(block, axis, route)


def widen(trial_rows, fetch_width):
    if fetch_width == 0:
        return trial_rows
    span_time = trial_rows.shape[-1]
    hop_count = min(-(-fetch_width // span_time), lax.axis_size("tm") - 1)
    pieces = [trial_rows]
    fetched = 0
    for hop_index in range(1, hop_count + 1):
        taken_cols = min(span_time, fetch_width - fetched)
        arrived = passed_along(trial_rows[..., span_time - taken_cols :], "tm", hop_index)
        pieces.insert(0, arrived)
        fetched = fetched + taken_cols
    if fetched < fetch_width:
        pieces.insert(
            0, jnp.zeros(trial_rows.shape[:-1] + (fetch_width - fetched,), trial_rows.dtype)
        )
    return jnp.concatenate(pieces, axis=-1)


def align_pair(low_set, high_set, margin, need_now, fetch_width):
    if fetch_width == 0:
        return (low_set[..., need_now:], high_set, margin - need_now)
    high_set = widen(high_set, fetch_width)
    low_set = widen(low_set, fetch_width - need_now)
    return (low_set, high_set, fetch_width - need_now)


def delay_of(trial_ids, subband_ids, trial_count, low_share, jitter):
    all_trials = low_share.shape[0] + 1
    rate_rows = jnp.take(low_share, all_trials // trial_count - 1 + subband_ids)
    return (trial_ids * rate_rows + jnp.take(jitter, trial_count - 2 + trial_ids)) // 64


def merge_rows(low_rows, high_rows, shifts, need_now):
    offsets = need_now - shifts
    bit_count = max(need_now.bit_length(), 1)
    moved = high_rows
    for bit_index in range(bit_count):
        step_size = 2**bit_index
        cols = moved.shape[-1]
        selected = (offsets >> bit_index & 1)[:, None] == 1
        moved = jnp.where(selected, moved[:, step_size:], moved[:, : cols - step_size])
    return low_rows + moved


def shards_any_reach(spectrogram, low_share, jitter):
    trial_dev = spectrogram.shape[0] // SUMMED
    span_time = spectrogram.shape[1]
    all_trials = low_share.shape[0] + 1
    freq_bits = lax.axis_size("freq").bit_length() - 1
    device = lax.axis_index("freq")
    local_counts = []
    trial_count = 2
    while trial_count <= trial_dev:
        local_counts.append(trial_count)
        trial_count = trial_count * 2
    cross_counts = [trial_dev * 2 ** (bit_index + 1) for bit_index in range(freq_bits)]
    need_list = [count_now - 1 for count_now in local_counts + cross_counts] + [
        2 ** (WIDTHS - 1) - 1
    ]
    fetch_plan = []
    margin = 0
    for position in range(len(need_list)):
        need_now = need_list[position]
        if margin >= need_now:
            fetch_plan.append(0)
            margin = margin - need_now
            continue
        fetch_width = need_now
        for later_need in need_list[position + 1 :]:
            if fetch_width + later_need > span_time:
                break
            fetch_width = fetch_width + later_need
        fetch_plan.append(fetch_width)
        margin = fetch_width - need_now
    states = jnp.sum(spectrogram.reshape(trial_dev, SUMMED, span_time), axis=1, dtype=jnp.float32)[
        :, None, :
    ]
    margin = 0
    section_index = 0
    for trial_count in local_counts:
        need_now = trial_count - 1
        groups = states.shape[0] // 2
        low_set, high_set, margin = align_pair(
            states[0::2], states[1::2], margin, need_now, fetch_plan[section_index]
        )
        low_rows = jnp.repeat(low_set, 2, axis=1).reshape(groups * trial_count, -1)
        high_rows = jnp.repeat(high_set, 2, axis=1).reshape(groups * trial_count, -1)
        trial_ids = jnp.tile(jnp.arange(trial_count, dtype=jnp.int32), groups)
        subband_ids = device * (trial_dev // trial_count) + jnp.repeat(
            jnp.arange(groups, dtype=jnp.int32), trial_count
        )
        shifts = delay_of(trial_ids, subband_ids, trial_count, low_share, jitter)
        states = merge_rows(low_rows, high_rows, shifts, need_now).reshape(groups, trial_count, -1)
        section_index = section_index + 1
    trial_rows = states[0]
    trial_ids = jnp.arange(trial_dev, dtype=jnp.int32)
    for bit_index in range(freq_bits):
        trial_count = cross_counts[bit_index]
        need_now = trial_count - 1
        partner = swapped(trial_rows, "freq", bit_index)
        upper_half = device >> bit_index & 1
        low_rows = jnp.where(upper_half == 1, partner, trial_rows)
        high_rows = jnp.where(upper_half == 1, trial_rows, partner)
        low_rows, high_rows, margin = align_pair(
            low_rows, high_rows, margin, need_now, fetch_plan[section_index]
        )
        trial_ids = 2 * trial_ids + upper_half
        shifts = delay_of(trial_ids, device >> bit_index + 1, trial_count, low_share, jitter)
        trial_rows = merge_rows(low_rows, high_rows, shifts, need_now)
        section_index = section_index + 1
    if fetch_plan[section_index] > 0:
        trial_rows = widen(trial_rows, fetch_plan[section_index])
    signal = trial_rows / math.sqrt(all_trials * SUMMED)
    peak_rows = []
    window_sum = signal
    width_now = 1
    for level_index in range(WIDTHS):
        length = window_sum.shape[1]
        peak_rows.append(
            jnp.max(window_sum[:, length - span_time :], axis=0) / math.sqrt(width_now)
        )
        if level_index + 1 < WIDTHS:
            window_sum = window_sum[:, width_now:] + window_sum[:, : length - width_now]
            width_now = width_now * 2
    local_best = jnp.stack(peak_rows)
    return lax.pmax(local_best, "freq")


def moved(row, above, delay, lane):
    return pltpu.roll(jnp.where(lane >= LANES - delay, above, row), delay, 1)


def delays_of(subbands, trials, count, first_trial, first_subband, all_trials, share, rest):
    jitters = [rest[count - 2 + first_trial + j] for j in range(trials)]
    delays = []
    for s in range(subbands):
        rate = share[all_trials // count - 1 + first_subband + s]
        delays.append([((first_trial + j) * rate + jitters[j]) >> 6 for j in range(trials)])
    return delays


def merged(old, delays, lane):
    new = []
    for s in range(len(old) // 2):
        highs = [(row, pltpu.roll(row, 1, 0)) for row in old[2 * s + 1]]
        new.append(
            [
                old[2 * s][j // 2] + moved(*highs[j // 2], delays[s][j], lane)
                for j in range(2 * len(highs))
            ]
        )
    return new


def search(
    bands, slots, all_trials, cuts,
    spec_hbm, share_hbm, rest_hbm, best_ref,
    spec, share, rest, later_delays, base_rows, rows, here, before, part, parts,
    in_sem, sems, part_sems,
):
    k, m = lax.axis_index("freq"), lax.axis_index("tm")
    span = spec.shape[1]
    chunks = span // LANES
    local = spec.shape[0] // SUMMED
    each = local // bands

    half = local // 2
    spec_loads = []
    for i in range(2):
        channels = pl.ds(i * half * SUMMED, half * SUMMED)
        spec_loads.append(
            pltpu.make_async_copy(spec_hbm.at[channels], spec.at[channels], in_sem.at[i])
        )
    table_loads = [
        pltpu.make_async_copy(share_hbm, share, in_sem.at[2]),
        pltpu.make_async_copy(rest_hbm, rest, in_sem.at[3]),
    ]
    for load in spec_loads + table_loads:
        load.start()

    barrier = pltpu.get_barrier_semaphore()
    for j in range(1, bands):
        pl.semaphore_signal(
            barrier, inc=1, device_id=(lax.rem(k + j, bands), m), device_id_type=MESH
        )

    @pl.when(m > 0)
    def _():
        for j in range(bands):
            pl.semaphore_signal(
                barrier, inc=1, device_id=(lax.rem(k + j, bands), m - 1), device_id_type=MESH
            )

    lane = lax.broadcasted_iota(jnp.int32, (SUBLANES, LANES), 1)
    base_rows[...] = jnp.zeros_like(base_rows)

    @pl.when(m == 0)
    def _():
        before[...] = jnp.zeros_like(before)

    row_of = lax.broadcasted_iota(jnp.int32, (half, half * SUMMED), 0)
    channel = lax.broadcasted_iota(jnp.int32, (half, half * SUMMED), 1)
    ones = jnp.where(channel // SUMMED == row_of, 1.0, 0.0).astype(jnp.bfloat16)
    for i in range(2):
        spec_loads[i].wait()
        base = jnp.dot(
            ones,
            spec[i * half * SUMMED : (i + 1) * half * SUMMED],
            preferred_element_type=jnp.float32,
        )
        for q in range(chunks):
            base_rows[i * half : (i + 1) * half, q, :] = base[:, q * LANES : (q + 1) * LANES]
    for load in table_loads:
        load.wait()
    state = [[base_rows[s]] for s in range(local)]
    count = 2
    while count <= local:
        groups = local // count
        delays = delays_of(groups, count, count, 0, k * groups, all_trials, share, rest)
        state = merged(state, delays, lane)
        count = count * 2
    for d in range(local):
        rows[d] = state[0][d][: chunks + 1]

    @pl.when(m < slots - 1)
    def _():
        pl.semaphore_wait(barrier, 2 * bands - 1)

    @pl.when(m == slots - 1)
    def _():
        pl.semaphore_wait(barrier, bands - 1)

    kept = pl.ds(0, chunks)

    def here_copy(j):
        to = lax.rem(k + j, bands)
        return pltpu.make_async_remote_copy(
            src_ref=rows.at[pl.ds(to * each, each), kept], dst_ref=here.at[k, :, kept],
            send_sem=sems.at[0], recv_sem=sems.at[1],
            device_id=(to, m), device_id_type=MESH,
        )

    def next_copy(j):
        to = lax.rem(k + j, bands)
        return pltpu.make_async_remote_copy(
            src_ref=rows.at[pl.ds(to * each, each)], dst_ref=before.at[k],
            send_sem=sems.at[2], recv_sem=sems.at[3],
            device_id=(to, m + 1), device_id_type=MESH,
        )

    def all_of(blocks, sem):
        return pltpu.make_async_remote_copy(
            src_ref=blocks, dst_ref=blocks, send_sem=sem, recv_sem=sem,
            device_id=(k, m), device_id_type=MESH,
        )

    others = pl.ds(0, bands - 1)
    order = sorted(range(bands), key=lambda j: -min(j, bands - j))

    for j in order:
        if j > 0:
            here_copy(j).start()

    @pl.when(m < slots - 1)
    def _():
        for j in order:
            next_copy(j).start()

    here[k, :, :chunks] = rows[pl.ds(k * each, each), :chunks]

    levels = []
    width, groups, flat = each, bands, 0
    while count <= all_trials:
        width, groups = width * 2, groups // 2
        level = delays_of(groups, width, count, k * width, 0, all_trials, share, rest)
        for s in range(groups):
            for j in range(width):
                later_delays[flat + s * width + j] = level[s][j]
        levels.append((groups, width, flat))
        flat = flat + groups * width
        count = count * 2

    all_of(here.at[others, :, kept], sems.at[1]).wait_recv()

    @pl.when(m > 0)
    def _():
        all_of(before, sems.at[3]).wait_recv()

    state = []
    for s in range(bands):
        trials = []
        for i in range(each):
            own, old = here[s, i, :chunks], before[s, i]
            joint = own[:1] + old[chunks:]
            trials.append(jnp.concatenate([old[:chunks], joint, own[1:]], axis=0))
        state.append(trials)
    for groups, width, flat in levels:
        delays = [[later_delays[flat + s * width + j] for j in range(width)] for s in range(groups)]
        state = merged(state, delays, lane)

    def part_copy(j, i):
        span_rows = pl.ds(cuts[i], cuts[i + 1] - cuts[i])
        return pltpu.make_async_remote_copy(
            src_ref=part.at[span_rows], dst_ref=parts.at[k, span_rows],
            send_sem=part_sems.at[0, i], recv_sem=part_sems.at[1, i],
            device_id=(lax.rem(k + j, bands), m), device_id_type=MESH,
        )

    def part_of_others(i):
        return parts.at[others, pl.ds(cuts[i], cuts[i + 1] - cuts[i])]

    window = state[0]
    sent = 0
    used = WIDTHS * chunks
    for level in range(WIDTHS):
        w = 2**level
        peak = functools.reduce(jnp.maximum, window)[chunks:]
        part[level * chunks : (level + 1) * chunks] = peak * (
            1.0 / math.sqrt(all_trials * SUMMED * w)
        )
        if (level + 1) * chunks == cuts[sent + 1] or level + 1 == WIDTHS:
            for j in order:
                if j > 0:
                    part_copy(j, sent).start()
            sent = sent + 1
        if level + 1 < WIDTHS:
            later = []
            for row in window:
                above = pltpu.roll(row, 1, 0)
                if w < LANES:
                    above = moved(row, above, w, lane)
                later.append(row + above)
            window = later
    all_of(here.at[others, :, kept], sems.at[0]).wait_send()

    @pl.when(m < slots - 1)
    def _():
        all_of(before, sems.at[2]).wait_send()

    parts[k] = part[...]
    for i in range(len(cuts) - 1):
        all_of(part_of_others(i), part_sems.at[1, i]).wait_recv()
        best = functools.reduce(
            jnp.maximum, [parts[s, cuts[i] : cuts[i + 1]] for s in range(bands)]
        )
        for flat in range(cuts[i], min(cuts[i + 1], used)):
            at = flat % chunks * LANES
            best_ref[flat // chunks : flat // chunks + 1, at : at + LANES] = best[
                flat - cuts[i] : flat - cuts[i] + 1
            ]
    for i in range(len(cuts) - 1):
        all_of(part_of_others(i), part_sems.at[0, i]).wait_send()


def one_block_back(mesh, channels, span, all_trials):
    bands = mesh.shape["freq"]
    local = channels // bands // SUMMED
    if span * 2 != SUBLANES * LANES or all_trials > LANES or local % bands != 0:
        return False
    reach = sum(2**level - 1 for level in range(1, all_trials.bit_length()))
    return reach + 2 ** (WIDTHS - 1) - 1 <= span


def shards_one_back(bands, slots, spectrogram, low_share, jitter):
    depth, span = spectrogram.shape
    all_trials = low_share.shape[0] + 1
    local = depth // SUMMED
    chunks = span // LANES
    each = local // bands
    cuts = (0, WIDTHS * chunks)
    vmem = lambda *shape: pltpu.VMEM(shape, jnp.float32)
    return pl.pallas_call(
        functools.partial(search, bands, slots, all_trials, cuts),
        out_shape=jax.ShapeDtypeStruct((WIDTHS, span), jnp.float32),
        in_specs=[pl.BlockSpec(memory_space=pltpu.HBM)] * 3,
        out_specs=pl.BlockSpec(memory_space=pltpu.VMEM),
        scratch_shapes=[
            pltpu.VMEM((depth, span), spectrogram.dtype),
            pltpu.SMEM(low_share.shape, jnp.int32),
            pltpu.SMEM(jitter.shape, jnp.int32),
            pltpu.SMEM((all_trials,), jnp.int32),
            vmem(local, SUBLANES, LANES),
            vmem(local, chunks + 1, LANES),
            vmem(bands, each, chunks + 1, LANES),
            vmem(bands, each, chunks + 1, LANES),
            vmem(cuts[-1], LANES),
            vmem(bands, cuts[-1], LANES),
            pltpu.SemaphoreType.DMA((4,)),
            pltpu.SemaphoreType.DMA((4,)),
            pltpu.SemaphoreType.DMA((2, len(cuts) - 1)),
        ],
        compiler_params=pltpu.CompilerParams(collective_id=0, has_side_effects=True),
    )(spectrogram, low_share, jitter)


def solution(mesh):
    placed = (P("freq", "tm"), P(), P())
    bands, slots = mesh.shape["freq"], mesh.shape["tm"]

    def run(spectrogram, low_share, jitter):
        channels, time = spectrogram.shape
        body = shards_any_reach
        if one_block_back(mesh, channels, time // slots, low_share.shape[0] + 1):
            body = functools.partial(shards_one_back, bands, slots)
        return jax.shard_map(
            body, mesh=mesh, in_specs=placed, out_specs=P(None, "tm"), check_vma=False
        )(spectrogram, low_share, jitter)

    return run
```
